256 devices in a mesh: group: 16 (over z_hi, y), head: 16 (over x, z_lo, core).
Axes of the slice: x: 4, y: 4, z: 8 (z_hi: 4, z_lo: 2; z = z_hi * 2 + z_lo), core: 2. Of those that a mesh axis runs over, the one named last changes fastest.
Arguments:
- old_pool: bfloat16 [768, 256, 576], P('group', 'head'), may hold values from -6 to 6
- mig_source: int32 [16, 16, 1], replicated, may hold values from 0 to 15; in each aligned block of 16 rows (0 to 15, 16 to 31, ..., all dimensions but the last counted through in order) at most 2 rows name the same one
- mig_page: int32 [16, 16], replicated, may hold values from 0 to 47
- page_table: int32 [16, 64], P('group'), may hold values from 0 to 63, each once within a row
- lengths: int32 [256], P('group'), may hold values from 1 to 1024
- queries: bfloat16 [256, 2, 128, 576], P('group', None, 'head'), may hold values from -300 to 300
- new_latent: bfloat16 [256, 2, 576], P('group'), may hold values from -6 to 6
- w_uv: bfloat16 [128, 512, 128], P('head'), may hold values from -0.25 to 0.25
- w_out: bfloat16 [16384, 4096], P(None, 'head'), may hold values from -0.046875 to 0.046875
Outputs:
- projected: bfloat16 [256, 2, 4096], P('group', None, 'head')
The draws below stay inside these ranges and needn't reach their ends.
Inputs may be any that keep to these rules, and one draw needn't show every extreme that they name: `mig_source`: among the 16 slots of one destination group no source group is named more than 2 times; in some destination group one source is named exactly 2 times. `page_table`: each row is a permutation of the 64 pages of its group's pool.
All inputs are finite; a program needn't handle non-finite values.
Results may differ from the reference program's by a relative error of at most 0.015.
Values may be sent and summed in bfloat16 or wider, within the bound.
A program may use at most 128 MiB of HBM per device.

```python
import math
import jax
import jax.numpy as jnp
import numpy as np
from jax import lax

H = 128
KVR = 512
ROPE = 64
VD = 128
DW = 4096
PAGE = 256
PAGES_SEQ = 4
SEQS = 16
CAP = 2
LAT = 576
GROUPS = 16
TOTAL_SEQ = 256
POOL = 64
MIG = 16
OWN = 48
CTX = 1024


def draw_queries(key, part):
    key = jax.random.fold_in(key, 11)
    first = jax.random.fold_in(key, 0)
    values = jnp.clip(jax.random.normal(first, (TOTAL_SEQ, 2, H, LAT), jnp.float32), -6.0, 6.0)
    return values.astype(jnp.bfloat16)


def draw_new_latent(key, part):
    key = jax.random.fold_in(key, 12)
    values = jnp.clip(jax.random.normal(key, (TOTAL_SEQ, 2, LAT), jnp.float32), -6.0, 6.0)
    return values.astype(jnp.bfloat16)


def plant(values, stream_key, least, high):
    shape = values.shape
    index_at = [jax.random.randint(jax.random.fold_in(stream_key, axis), (), 0, shape[axis]) for axis in range(len(shape))]
    values = values.at[tuple(index_at)].set(least)
    longest = shape.index(max(shape))
    index_at[longest] = (index_at[longest] + 1) % shape[longest]
    return values.at[tuple(index_at)].set(high)


def steps_of(own_key, dims, pieces, smallest, top_value):
    loudness = 1.0
    for axis_at, shards_of in pieces:
        steps = jax.random.uniform(jax.random.fold_in(jax.random.fold_in(own_key, 6), axis_at), (shards_of,), jnp.float32, smallest / len(pieces), top_value / len(pieces))
        loudness = loudness * jnp.repeat(jnp.exp(steps), dims[axis_at] // shards_of).reshape((-1,) + (1,) * (len(dims) - 1 - axis_at))
    return loudness


def shared_out(own_key, own, number, rows, amount, top, bound, skew):
    sequence = jax.random.permutation(own_key, amount)
    heavy_load, common = portions_of(amount, rows * top, bound, skew, True), portions_of(amount, rows * top, bound, skew, False)
    places = jnp.arange(amount)

    def named(sizes, turn):
        used = int((sizes > 0).sum())
        fixed = max(1, used // 4)
        shifted = fixed + (places - fixed + turn * (used - fixed)) % max(1, amount - fixed)
        return jnp.zeros((amount,), jnp.int32).at[sequence[jnp.where(places < fixed, places, shifted)]].set(jnp.asarray(sizes, jnp.int32))

    sizes = jnp.where(number % 4 == 0, named(heavy_load, number // 4), named(common, number - number // 4 - 1))
    mixed = jax.random.permutation(jax.random.fold_in(own, 3), amount)
    donor, receiver = mixed[0:amount // 2 * 2:2], mixed[1:amount // 2 * 2:2]
    margin = jnp.minimum(sizes[donor] - 1, bound - sizes[receiver]) // 2
    margin = jnp.where((donor == sequence[0]) | (receiver == sequence[0]) | (sizes[receiver] == 0), 0, jnp.maximum(margin, 0))
    shifted = jax.random.randint(jax.random.fold_in(own, 4), (amount // 2,), 0, 1 << 20) % (margin + 1)
    sizes = sizes.at[donor].add(-shifted).at[receiver].add(shifted)
    labels = jnp.searchsorted(jnp.cumsum(sizes), jnp.arange(rows * top), side="right").astype(jnp.int32)
    listing = labels.reshape(top, rows).T
    listing = listing[jax.random.permutation(jax.random.fold_in(own, 1), rows)]
    turn = jax.random.randint(jax.random.fold_in(own, 2), (rows, 1), 0, top)
    return jnp.take_along_axis(listing, (jnp.arange(top)[None, :] + turn) % top, axis=1)


def portions_of(count, total, reach, lean, full):
    weights = [(1 << 20) // math.isqrt(standing ** lean) + 1 for standing in range(1, count + 1)]
    largest = reach if full else min(reach, max(-(-total // count), total * weights[0] // sum(weights)))
    least = 1 if total - largest >= count - 1 else 0
    holding, spare = [largest] + [least] * (count - 1), total - largest - least * (count - 1)
    while spare > 0:
        movable = [i for i in range(1, count) if holding[i] < largest] or [i for i in range(1, count) if holding[i] < reach]
        whole, budget = sum([weights[i] for i in movable]), spare
        for i in movable:
            extra = min(reach - holding[i], max(1, budget * weights[i] // whole), spare)
            holding[i] = holding[i] + extra
            spare = spare - extra
    return np.array(holding)


def centred(own_key, shape, spread, most, pieces=(), held_as=jnp.bfloat16):
    gain = steps_of(own_key, shape, pieces, -0.22, 0.18) if pieces else 1.0
    entries = jax.random.normal(own_key, shape, jnp.float32) * spread * gain
    return jnp.minimum(jnp.maximum(entries, -most), most).astype(held_as)


def setup_inputs(seed: int = 0) -> dict:
    seeds = jax.random.split(jax.random.key(seed), 10)
    old_pool = centred(seeds[0], (GROUPS * OWN, PAGE, LAT), 1.0, 6.0, ((0, 16), (1, 16)))
    mig_source_keys = jax.random.split(jax.random.fold_in(seeds[1], 1), GROUPS * MIG // MIG)
    mig_source_turns = jax.random.permutation(jax.random.fold_in(seeds[1], 3), GROUPS * MIG // MIG)
    mig_source = jax.vmap(lambda own, number: shared_out(jax.random.fold_in(seeds[1], 2), own, number, MIG, GROUPS, 1, CAP, 2))(mig_source_keys, mig_source_turns).reshape((GROUPS, MIG, 1))
    mig_page = plant(jax.random.randint(seeds[2], (GROUPS, MIG), 0, OWN), jax.random.fold_in(seeds[2], 1), 0, OWN - 1).astype(jnp.int32)
    page_table = jax.vmap(lambda own: jax.random.permutation(own, POOL))(jax.random.split(seeds[3], GROUPS)).reshape((GROUPS, POOL)).astype(jnp.int32)
    lengths = plant(jax.random.randint(seeds[4], (TOTAL_SEQ,), 1, CTX + 1), jax.random.fold_in(seeds[4], 1), 1, CTX).astype(jnp.int32)
    queries = draw_queries(jax.random.fold_in(seeds[9], 71), 0)
    new_latent = draw_new_latent(jax.random.fold_in(seeds[9], 71), 0)
    w_uv = centred(seeds[7], (H, KVR, VD), KVR ** -0.5, 0.25, ((0, 16),))
    w_out = centred(seeds[8], (H * VD, DW), (H * VD) ** -0.5, 0.046875, ((1, 16),))
    return {"old_pool": old_pool, "mig_source": mig_source, "mig_page": mig_page, "page_table": page_table, "lengths": lengths, "queries": queries, "new_latent": new_latent, "w_uv": w_uv, "w_out": w_out}


def reference(old_pool, mig_source, mig_page, page_table, lengths, queries, new_latent, w_uv, w_out):
    pools = old_pool.reshape(GROUPS, OWN, PAGE, LAT)
    source = mig_source[:, :, 0]
    incoming = pools[source, mig_page]
    fresh = jnp.concatenate([pools, incoming], axis=1)
    tables = page_table.reshape(GROUPS, SEQS, PAGES_SEQ)
    query_all = queries.reshape(GROUPS, SEQS, 2, H, LAT)
    newest = new_latent.reshape(GROUPS, SEQS, 2, LAT)
    length_all = lengths.reshape(GROUPS, SEQS)
    scale = (VD + ROPE) ** -0.5
    causal = jnp.arange(2)[None, :] <= jnp.arange(2)[:, None]

    def one_group(packed):
        pool, table, query, latest, length = packed
        key_rows = jnp.take(pool, table, axis=0).reshape(SEQS, CTX, LAT)
        key_all = jnp.concatenate([key_rows, latest], axis=1)
        cached = jnp.arange(CTX)[None, :] < length[:, None]
        cached = jnp.broadcast_to(cached[:, None, :], (SEQS, 2, CTX))
        fresh_seen = jnp.broadcast_to(causal[None, :, :], (SEQS, 2, 2))
        visible = jnp.concatenate([cached, fresh_seen], axis=2)[:, :, None, :]
        scores = jnp.einsum("sthc,slc->sthl", query.astype(jnp.float32), key_all.astype(jnp.float32)) * scale
        scores = jnp.where(visible, scores, -1e30)
        highest = jnp.max(scores, axis=3, keepdims=True)
        weights = jnp.where(visible, jnp.exp(scores - highest), 0.0)
        total = jnp.sum(weights, axis=3)
        rounded = weights.astype(jnp.bfloat16).astype(jnp.float32)
        summed = jnp.einsum("sthl,slc->sthc", rounded, key_all[:, :, :KVR].astype(jnp.float32))
        latent = (summed / total[..., None]).astype(jnp.bfloat16)
        head_values = jnp.einsum("sthc,hcv->sthv", latent.astype(jnp.float32), w_uv.astype(jnp.float32)).astype(jnp.bfloat16)
        flattened = head_values.reshape(SEQS * 2, H * VD)
        result = jnp.dot(flattened, w_out, preferred_element_type=jnp.float32).astype(jnp.bfloat16)
        return result.reshape(SEQS, 2, DW)

    outputs = lax.map(one_group, (fresh, tables, query_all, newest, length_all))
    return outputs.reshape(TOTAL_SEQ, 2, DW)
```

```python
import functools

import jax
import jax.numpy as jnp
from jax import lax
from jax.experimental import pallas as pl
from jax.experimental.pallas import tpu as pltpu
from jax.sharding import PartitionSpec as P

KVR = 512
ROPE = 64
VD = 128
CAP = 2
MESH = pl.DeviceIdType.MESH
HIDDEN = -1e30


def kernel(
    dims,
    source_ref,
    page_ref,
    table_ref,
    length_ref,
    pool_hbm,
    query_hbm,
    new_ref,
    w_uv_hbm,
    w_out_hbm,
    out_ref,
    pool,
    pages,
    mig_out,
    keys,
    kv_out,
    queries,
    scores,
    lat_out,
    lat_in,
    values,
    w_uv,
    w_out,
    place,
    mig_send,
    mig_recv,
    q_send,
    q_recv,
    kv_send,
    kv_recv,
    lat_send,
    lat_recv,
    hv_send,
    hv_recv,
    local_sem,
):
    groups, heads, own, slots, rows, migrate, heads_each, page_len = dims
    my_group = lax.axis_index("group")
    me = lax.axis_index("head")
    lat = pool_hbm.shape[2]
    width = slots * rows
    lanes = heads * width

    pool_copy = pltpu.make_async_copy(pool_hbm, pool, local_sem.at[0])
    pool_copy.start()
    page_copy = pltpu.make_async_copy(pool_hbm, pages.at[pl.ds(0, own)], local_sem.at[4])
    page_copy.start()

    barrier = pltpu.get_barrier_semaphore()
    for d in range(1, groups):
        to = lax.rem(my_group + d, groups)
        pl.semaphore_signal(barrier, inc=1, device_id=(to, me), device_id_type=MESH)
    for d in range(1, heads):
        to = lax.rem(me + d, heads)
        pl.semaphore_signal(barrier, inc=1, device_id=(my_group, to), device_id_type=MESH)

    query_copy = pltpu.make_async_copy(query_hbm.at[me], queries.at[me], local_sem.at[1])
    query_copy.start()
    uv_copy = pltpu.make_async_copy(w_uv_hbm, w_uv, local_sem.at[2])
    uv_copy.start()
    out_copy = pltpu.make_async_copy(w_out_hbm, w_out, local_sem.at[3])
    out_copy.start()

    def wanted_by(group):
        first = jnp.int32(0)
        second = jnp.int32(0)
        for j in reversed(range(migrate)):
            mine = source_ref[group * migrate + j] == my_group
            page = page_ref[group * migrate + j]
            second = jnp.where(mine, first, second)
            first = jnp.where(mine, page, first)
        return first, second

    pool_copy.wait()
    first, second = wanted_by(my_group)
    pages[own + my_group * CAP] = pool[first]
    pages[own + my_group * CAP + 1] = pool[second]
    for d in range(1, groups):
        to = lax.rem(my_group + d, groups)
        first, second = wanted_by(to)
        mig_out[d, 0] = pool[first]
        mig_out[d, 1] = pool[second]

    pl.semaphore_wait(barrier, groups + heads - 2)

    mig_copies = []
    for d in range(1, groups):
        to = lax.rem(my_group + d, groups)
        copy = pltpu.make_async_remote_copy(
            src_ref=mig_out.at[d],
            dst_ref=pages.at[pl.ds(own + my_group * CAP, CAP)],
            send_sem=mig_send.at[d],
            recv_sem=mig_recv.at[d],
            device_id=(to, me),
            device_id_type=MESH,
        )
        copy.start()
        mig_copies.append(copy)
    q_copies = []
    for d in range(1, heads):
        to = lax.rem(me + d, heads)
        copy = pltpu.make_async_remote_copy(
            src_ref=query_hbm.at[to],
            dst_ref=queries.at[me],
            send_sem=q_send.at[d],
            recv_sem=q_recv.at[d],
            device_id=(my_group, to),
            device_id_type=MESH,
        )
        copy.start()
        q_copies.append(copy)

    for j in range(migrate):
        from_group = source_ref[my_group * migrate + j]
        rank = jnp.int32(0)
        for i in range(j):
            rank = rank + jnp.where(source_ref[my_group * migrate + i] == from_group, 1, 0)
        place[j] = own + from_group * CAP + rank

    spare = keys.shape[0] - lanes
    pick = (
        lax.broadcasted_iota(jnp.int32, (spare, 2 * heads), 1)
        == lax.broadcasted_iota(jnp.int32, (spare, 2 * heads), 0) + 2 * me
    ) & (lax.broadcasted_iota(jnp.int32, (spare, 2 * heads), 0) < 2)
    keys[pl.ds(lanes, spare)] = jnp.dot(
        jnp.where(pick, 1.0, 0.0).astype(jnp.bfloat16),
        new_ref[...].reshape(2 * heads, lat),
        preferred_element_type=jnp.float32,
    ).astype(jnp.bfloat16)

    page_copy.wait()
    for copy in mig_copies:
        copy.wait_recv()

    def fill(seq, store):
        for k in range(slots):
            page = table_ref[seq * slots + k]
            moved = place[jnp.maximum(page - own, 0)]
            store(k, pages[jnp.where(page < own, page, moved)])

    kv_copies = []
    for d in range(1, heads):
        to = lax.rem(me + d, heads)

        def to_outgoing(k, value, d=d):
            kv_out[d, pl.ds(k * rows, rows)] = value

        fill(to, to_outgoing)
        copy = pltpu.make_async_remote_copy(
            src_ref=kv_out.at[d],
            dst_ref=keys.at[pl.ds(pl.multiple_of(me * width, width), width)],
            send_sem=kv_send.at[d],
            recv_sem=kv_recv.at[d],
            device_id=(my_group, to),
            device_id_type=MESH,
        )
        copy.start()
        kv_copies.append(copy)

    def to_keys(k, value):
        keys[pl.ds(pl.multiple_of(me * width + k * rows, rows), rows)] = value

    fill(me, to_keys)

    query_copy.wait()
    for copy in q_copies:
        copy.wait_recv()
    for copy in kv_copies:
        copy.wait_recv()

    row_count = heads * 2 * heads_each
    query = queries[...].reshape(row_count, lat)
    scale = (VD + ROPE) ** (-0.5)
    length = length_ref[me]
    chunk = min(256, lanes)
    starts = list(range(0, lanes, chunk))

    def dot_keys(start, size):
        return (
            lax.dot_general(
                query,
                keys[start : start + size],
                (((1,), (1,)), ((), ())),
                preferred_element_type=jnp.float32,
            )
            * scale
        )

    column = lax.broadcasted_iota(jnp.int32, (row_count, spare), 1)
    token = lax.broadcasted_iota(jnp.int32, (row_count, spare), 0) // heads_each % 2
    new_scores = jnp.where(column <= token, dot_keys(lanes, spare), HIDDEN)
    highest = jnp.max(new_scores, axis=1, keepdims=True)
    for start in starts:
        entry = lax.broadcasted_iota(jnp.int32, (1, chunk), 1) + start
        position = (
            entry // rows % slots * page_len + entry // width * rows + entry % rows
        )
        shown = jnp.where(position < length, dot_keys(start, chunk), HIDDEN)
        scores[:, start : start + chunk] = shown
        highest = jnp.maximum(highest, jnp.max(shown, axis=1, keepdims=True))
    weights = jnp.exp(new_scores - highest)
    totals = jnp.sum(weights, axis=1, keepdims=True)
    weighted = jnp.dot(
        weights.astype(jnp.bfloat16), keys[lanes:, :KVR], preferred_element_type=jnp.float32
    )
    for start in starts:
        weights = jnp.exp(scores[:, start : start + chunk] - highest)
        totals = totals + jnp.sum(weights, axis=1, keepdims=True)
        weighted = weighted + jnp.dot(
            weights.astype(jnp.bfloat16),
            keys[start : start + chunk, :KVR],
            preferred_element_type=jnp.float32,
        )
    lat_out[...] = (weighted / totals).astype(jnp.bfloat16).reshape(lat_out.shape)

    lat_copies = []
    for d in range(1, heads):
        to = lax.rem(me + d, heads)
        copy = pltpu.make_async_remote_copy(
            src_ref=lat_out.at[to],
            dst_ref=lat_in.at[me],
            send_sem=lat_send.at[d],
            recv_sem=lat_recv.at[d],
            device_id=(my_group, to),
            device_id_type=MESH,
        )
        copy.start()
        lat_copies.append(copy)
    lat_in[me] = lat_out[me]
    uv_copy.wait()
    for copy in lat_copies:
        copy.wait_recv()

    seq_tokens = 2 * heads
    target = lax.broadcasted_iota(jnp.int32, (row_count, row_count), 0)
    origin = lax.broadcasted_iota(jnp.int32, (row_count, row_count), 1)
    permute = jnp.where(
        origin == target % seq_tokens * heads_each + target // seq_tokens, 1.0, 0.0
    ).astype(jnp.bfloat16)
    by_head = jnp.dot(
        permute, lat_in[...].reshape(row_count, KVR), preferred_element_type=jnp.float32
    ).astype(jnp.bfloat16)
    for n in range(heads_each):
        values[me, :, n * VD : (n + 1) * VD] = jnp.dot(
            by_head[n * seq_tokens : (n + 1) * seq_tokens],
            w_uv[n],
            preferred_element_type=jnp.float32,
        ).astype(jnp.bfloat16)

    hv_copies = []
    for d in range(1, heads):
        to = lax.rem(me + d, heads)
        copy = pltpu.make_async_remote_copy(
            src_ref=values.at[me],
            dst_ref=values.at[me],
            send_sem=hv_send.at[d],
            recv_sem=hv_recv.at[d],
            device_id=(my_group, to),
            device_id_type=MESH,
        )
        copy.start()
        hv_copies.append(copy)
    out_copy.wait()
    depth = heads_each * VD

    def block(h):
        return jnp.dot(
            values[h],
            w_out[pl.ds(pl.multiple_of(h * depth, depth), depth)],
            preferred_element_type=jnp.float32,
        )

    result = block(me)
    for d in range(1, heads):
        hv_copies[d - 1].wait_recv()
        result = result + block(lax.rem(me - d + heads, heads))
    out_ref[...] = result.astype(out_ref.dtype)

    for copy in mig_copies + q_copies + kv_copies + lat_copies + hv_copies:
        copy.wait_send()


def shards(old_pool, mig_source, mig_page, page_table, lengths, queries, new_latent, w_uv, w_out):
    groups = lax.axis_size("group")
    heads = lax.axis_size("head")
    own, rows, lat = old_pool.shape
    seqs, tokens, heads_each, _ = queries.shape
    migrate = mig_source.shape[1]
    slots = page_table.shape[1] // seqs
    features = w_out.shape[1]
    dims = (groups, heads, own, slots, rows, migrate, heads_each, rows * heads)
    lanes = heads * slots * rows
    spare = 128
    half = jnp.bfloat16
    smem = pl.BlockSpec(memory_space=pltpu.SMEM)
    anywhere = pl.BlockSpec(memory_space=pl.ANY)
    vmem = pl.BlockSpec(memory_space=pltpu.VMEM)
    dma = pltpu.SemaphoreType.DMA
    result = pl.pallas_call(
        functools.partial(kernel, dims),
        out_shape=jax.ShapeDtypeStruct((seqs * tokens, features), half),
        in_specs=[smem, smem, smem, smem, anywhere, anywhere, vmem, anywhere, anywhere],
        out_specs=vmem,
        scratch_shapes=[
            pltpu.VMEM((own, rows, lat), half),
            pltpu.VMEM((own + groups * CAP, rows, lat), half),
            pltpu.VMEM((groups, CAP, rows, lat), half),
            pltpu.VMEM((lanes + spare, lat), half),
            pltpu.VMEM((heads, slots * rows, lat), half),
            pltpu.VMEM((heads, tokens * heads_each, lat), half),
            pltpu.VMEM((heads * tokens * heads_each, lanes), jnp.float32),
            pltpu.VMEM((heads, tokens * heads_each, KVR), half),
            pltpu.VMEM((heads, tokens * heads_each, KVR), half),
            pltpu.VMEM((heads, seqs * tokens, heads_each * VD), half),
            pltpu.VMEM(w_uv.shape, half),
            pltpu.VMEM(w_out.shape, half),
            pltpu.SMEM((migrate,), jnp.int32),
            dma((groups,)),
            dma((groups,)),
            dma((heads,)),
            dma((heads,)),
            dma((heads,)),
            dma((heads,)),
            dma((heads,)),
            dma((heads,)),
            dma((heads,)),
            dma((heads,)),
            dma((5,)),
        ],
        compiler_params=pltpu.CompilerParams(
            collective_id=0, has_side_effects=True, vmem_limit_bytes=48 * 1024 * 1024
        ),
    )(
        mig_source.reshape(-1),
        mig_page.reshape(-1),
        page_table.reshape(-1),
        lengths,
        old_pool,
        queries.reshape(seqs, tokens * heads_each, lat),
        new_latent,
        w_uv,
        w_out,
    )
    return result.reshape(seqs, tokens, features)


def solution(mesh):
    return jax.shard_map(
        shards,
        mesh=mesh,
        in_specs=(
            P("group", "head", None),
            P(),
            P(),
            P("group", None),
            P("group"),
            P("group", None, "head", None),
            P("group", None, None),
            P("head", None, None),
            P(None, "head"),
        ),
        out_specs=P("group", None, "head"),
        check_vma=False,
    )
```

```python
import functools

import jax
import jax.numpy as jnp
from jax import lax
from jax.experimental import pallas as pl
from jax.experimental.pallas import tpu as pltpu
from jax.sharding import PartitionSpec as P

KVR = 512
ROPE = 64
VD = 128
CAP = 2
MESH = pl.DeviceIdType.MESH
HIDDEN = -1e30
CHUNKS = ((0, 128), (128, 128), (256, 128), (384, 128), (512, 64))


def kernel(
    dims,
    chunks,
    source_hbm,
    page_hbm,
    table_hbm,
    length_hbm,
    pool_hbm,
    query_hbm,
    new_hbm,
    w_uv_hbm,
    w_out_hbm,
    out_ref,
    source,
    page_of,
    table,
    length_of,
    place,
    new,
    new_keys,
    pool,
    queries,
    scores,
    lat_out,
    lat_in,
    values,
    w_uv,
    w_out,
    pages,
    mig_out,
    mig_in,
    keys,
    kv_out,
    kv_in,
    mig_send,
    mig_recv,
    q_send,
    q_recv,
    kv_send,
    kv_recv,
    lat_send,
    lat_recv,
    hv_send,
    hv_recv,
    local_sem,
):
    groups, heads, own, slots, rows, migrate, heads_each = dims
    my_group = lax.axis_index("group")
    me = lax.axis_index("head")
    columns = heads // 2
    part = lax.rem(me // 2, 2)
    column = me // 4 * 2 + lax.rem(me, 2)
    lat = pool_hbm.shape[2]
    width = slots * rows
    block_rows = 2 * width
    parts = range(len(chunks))
    last = len(chunks) - 1

    def device_of(col, half):
        return col // 2 * 4 + half * 2 + lax.rem(col, 2)

    barrier = pltpu.get_barrier_semaphore()
    for d in range(1, groups):
        to = lax.rem(my_group + d, groups)
        pl.semaphore_signal(barrier, inc=1, device_id=(to, me), device_id_type=MESH)
    for d in range(1, heads):
        to = lax.rem(me + d, heads)
        pl.semaphore_signal(barrier, inc=1, device_id=(my_group, to), device_id_type=MESH)

    def fetch(src, dst, n):
        copy = pltpu.make_async_copy(src, dst, local_sem.at[n])
        copy.start()
        return copy

    def remote(src, dst, send, recv, group, head):
        copy = pltpu.make_async_remote_copy(
            src_ref=src,
            dst_ref=dst,
            send_sem=send,
            recv_sem=recv,
            device_id=(group, head),
            device_id_type=MESH,
        )
        copy.start()
        return copy

    index_copies = [
        fetch(source_hbm, source, 0),
        fetch(page_hbm, page_of, 1),
        fetch(table_hbm, table, 2),
        fetch(length_hbm, length_of, 3),
    ]
    pool_copy = fetch(pool_hbm, pool, 4)
    new_copy = fetch(new_hbm, new, 5)
    query_copy = fetch(query_hbm.at[:, column], queries.at[me], 6)
    page_copies = [
        fetch(
            pool_hbm.at[:, :, pl.ds(start, size)], pages[c].at[pl.ds(0, own)], 9 + c
        )
        for c, (start, size) in enumerate(chunks)
    ]
    uv_copy = fetch(w_uv_hbm, w_uv, 7)
    out_copy = fetch(w_out_hbm, w_out, 8)

    def wanted_by(group):
        first = jnp.int32(0)
        second = jnp.int32(0)
        for j in reversed(range(migrate)):
            mine = source[group, 0, j] == my_group
            second = jnp.where(mine, first, second)
            first = jnp.where(mine, page_of[group, j], first)
        return first, second

    for copy in index_copies:
        copy.wait()
    pool_copy.wait()
    for d in range(groups):
        to = lax.rem(my_group + d, groups)
        first, second = (pool[page] for page in wanted_by(to))
        for c, (start, size) in enumerate(chunks[:last]):
            for r, value in enumerate((first, second)):
                cut = value[:, start : start + size]
                if d == 0:
                    pages[c][own + my_group * CAP + r] = cut
                else:
                    mig_out[c][d, r] = cut
        rotary = jnp.concatenate([first[:, KVR:], second[:, KVR:]], axis=1)
        if d == 0:
            mig_in[my_group] = rotary
        else:
            mig_out[last][d] = rotary

    pl.semaphore_wait(barrier, groups + heads - 2)

    def send_migration(c):
        copies = []
        for d in range(1, groups):
            to = lax.rem(my_group + d, groups)
            copies.append(
                remote(
                    mig_out[c].at[d],
                    pages[c].at[pl.ds(own + my_group * CAP, CAP)]
                    if c < last
                    else mig_in.at[my_group],
                    mig_send.at[c, d],
                    mig_recv.at[c, d],
                    to,
                    me,
                )
            )
        return copies

    def send_queries(half, first, n):
        copies = []
        for d in range(first, columns):
            col = lax.rem(column + d, columns)
            copies.append(
                remote(
                    query_hbm.at[:, col],
                    queries.at[me],
                    q_send.at[n, d],
                    q_recv.at[n, d],
                    my_group,
                    device_of(col, half),
                )
            )
        return copies

    mig_copies = [send_migration(0)]
    q_copies = send_queries(part, 1, 0)
    for c in parts[1:]:
        mig_copies.append(send_migration(c))

    for j in range(migrate):
        from_group = source[my_group, 0, j]
        rank = jnp.int32(0)
        for i in range(j):
            rank = rank + jnp.where(source[my_group, 0, i] == from_group, 1, 0)
        place[j] = own + from_group * CAP + rank

    new_copy.wait()
    spare = new_keys.shape[0]
    entry = lax.broadcasted_iota(jnp.int32, (spare, 2 * heads), 0)
    pick = (
        lax.broadcasted_iota(jnp.int32, (spare, 2 * heads), 1)
        == entry // 2 * heads + 2 * column + entry % 2
    ) & (entry < 4)
    new_keys[...] = jnp.dot(
        jnp.where(pick, 1.0, 0.0).astype(jnp.bfloat16),
        new[...].reshape(2 * heads, lat),
        preferred_element_type=jnp.float32,
    ).astype(jnp.bfloat16)

    def page_at(seq, k):
        page = table[0, seq * slots + k]
        return jnp.where(page < own, page, place[jnp.maximum(page - own, 0)])

    at = []
    for d in range(columns):
        col = lax.rem(column + d, columns)
        at.append([page_at(n // slots * columns + col, n % slots) for n in range(2 * slots)])

    kv_copies = []
    for c in parts:
        page_copies[c].wait()
        for copy in mig_copies[c]:
            copy.wait_recv()
        if c == last:
            for g in range(groups):
                for r in range(CAP):
                    pages[c][own + g * CAP + r] = mig_in[g, :, r * ROPE : (r + 1) * ROPE]

        def fill(block, d, c=c):
            if c < last:
                for n in range(2 * slots):
                    block[n * rows : (n + 1) * rows] = pages[c][at[d][n]]
                return
            for n in range(slots):
                k = n // 2 * slots + n % 2
                block[n * rows : (n + 1) * rows] = jnp.concatenate(
                    [pages[c][at[d][k]], pages[c][at[d][k + 2]]], axis=1
                )

        landing = keys[c] if c < last else kv_in
        copies = []
        for d in range(1, columns):
            fill(kv_out[c].at[d], d)
            copies.append(
                remote(
                    kv_out[c].at[d],
                    landing.at[column],
                    kv_send.at[c, d],
                    kv_recv.at[c, d],
                    my_group,
                    device_of(lax.rem(column + d, columns), part),
                )
            )
        fill(landing.at[column], 0)
        kv_copies.append(copies)
        if c == 1:
            q_copies = q_copies + send_queries(1 - part, 0, 1)

    row_count = heads * 2 * heads_each
    lanes = columns * width
    scale = (VD + ROPE) ** (-0.5)

    query_copy.wait()
    for copy in q_copies:
        copy.wait_recv()

    def dot_keys(s, start, size, key_rows):
        return lax.dot_general(
            queries[:, s, :, start : start + size].reshape(row_count, size),
            key_rows,
            (((1,), (1,)), ((), ())),
            preferred_element_type=jnp.float32,
        )

    def key_rows(c, s, size):
        return keys[c][:, s * width : (s + 1) * width, :size].reshape(lanes, size)

    for c, (start, size) in enumerate(chunks):
        for copy in kv_copies[c]:
            copy.wait_recv()
        if c == last:
            for col in range(columns):
                for n in range(4):
                    keys[c][col, n * 2 * rows : (n + 1) * 2 * rows] = kv_in[
                        col,
                        n // 2 * 2 * rows : (n // 2 + 1) * 2 * rows,
                        n % 2 * ROPE : (n % 2 + 1) * ROPE,
                    ]
        for s in range(2):
            some = dot_keys(s, start, size, key_rows(c, s, size))
            scores[s] = some if c == 0 else scores[s] + some

    number = lax.broadcasted_iota(jnp.int32, (1, lanes), 1)
    from_column = number // width
    position = (
        number // rows % slots * (rows * heads)
        + device_of(from_column, part) * rows
        + number % rows
    )
    new_column = lax.broadcasted_iota(jnp.int32, (row_count, spare), 1)
    token = lax.broadcasted_iota(jnp.int32, (row_count, spare), 0) // heads_each % 2
    stat_lane = lax.broadcasted_iota(jnp.int32, (row_count, 128), 1)

    def in_three(value):
        out = []
        for _ in range(3):
            top = value.astype(jnp.bfloat16).astype(jnp.float32)
            out.append(top)
            value = value - top
        return out

    mine_at = part * columns + column
    lat_copies = []
    for s in range(2):
        new_shown = (
            (new_column >= 2 * s) & (new_column - 2 * s <= token) & (new_column < 2 * s + 2)
        ) & (part == 0)
        new_scores = jnp.where(
            new_shown, dot_keys(s, 0, lat, new_keys[...]) * scale, HIDDEN
        )
        shown = jnp.where(position < length_of[s * columns + column], scores[s] * scale, HIDDEN)
        highest = jnp.maximum(
            jnp.max(new_scores, axis=1, keepdims=True), jnp.max(shown, axis=1, keepdims=True)
        )
        new_weights = jnp.exp(new_scores - highest)
        weights = jnp.exp(shown - highest)
        totals = jnp.sum(new_weights, axis=1, keepdims=True) + jnp.sum(
            weights, axis=1, keepdims=True
        )
        new_weights = new_weights.astype(jnp.bfloat16)
        weights = weights.astype(jnp.bfloat16)
        for c, (start, size) in enumerate(chunks):
            size = min(size, KVR - start)
            if size > 0:
                weighted = jnp.dot(
                    weights, key_rows(c, s, size), preferred_element_type=jnp.float32
                ) + jnp.dot(
                    new_weights,
                    new_keys[:, start : start + size],
                    preferred_element_type=jnp.float32,
                )
                lat_out[s, :, :, start : start + size] = (
                    (weighted / totals).astype(jnp.bfloat16).reshape(heads, -1, size)
                )
        stats = jnp.zeros((row_count, 128), jnp.float32)
        for n, piece in enumerate(in_three(highest) + in_three(totals)):
            stats = jnp.where(stat_lane == n, piece, stats)
        lat_out[s, :, :, KVR:] = stats.astype(jnp.bfloat16).reshape(heads, -1, 128)
        copies = []
        for d in range(1, heads):
            to = lax.rem(me + d, heads)
            copies.append(
                remote(
                    lat_out.at[s, to],
                    lat_in.at[s, mine_at],
                    lat_send.at[s, d],
                    lat_recv.at[s, d],
                    my_group,
                    to,
                )
            )
        lat_in[s, mine_at] = lat_out[s, me]
        lat_copies.append(copies)

    half_tokens = 2 * columns
    half_rows = half_tokens * heads_each
    target = lax.broadcasted_iota(jnp.int32, (half_rows, half_rows), 0)
    origin = lax.broadcasted_iota(jnp.int32, (half_rows, half_rows), 1)
    by_head = jnp.where(
        origin == target % half_tokens * heads_each + target // half_tokens, 1.0, 0.0
    ).astype(jnp.bfloat16)

    chips = heads // 2
    my_chip, core = me // 2, lax.rem(me, 2)
    sibling = my_chip * 2 + 1 - core

    def hand_on(s, h, to, n):
        return remote(
            values.at[s, h],
            values.at[s, h],
            hv_send.at[s, n],
            hv_recv.at[s, n],
            my_group,
            to,
        )

    uv_copy.wait()
    hv_copies = []
    passed = []
    for s in range(2):
        for copy in lat_copies[s]:
            copy.wait_recv()
        stat = []
        for z in range(2):
            tile = lat_in[s, z * columns : (z + 1) * columns, :, KVR:]
            stat.append(tile.reshape(half_rows, 128).astype(jnp.float32))

        def joined(z, n):
            return stat[z][:, n : n + 1] + stat[z][:, n + 1 : n + 2] + stat[z][:, n + 2 : n + 3]

        peaks = [joined(z, 0) for z in range(2)]
        top = jnp.maximum(peaks[0], peaks[1])
        shares = [joined(z, 3) * jnp.exp(peaks[z] - top) for z in range(2)]
        whole = shares[0] + shares[1]
        merged = sum(
            lat_in[s, z * columns : (z + 1) * columns, :, :KVR]
            .reshape(half_rows, KVR)
            .astype(jnp.float32)
            * (shares[z] / whole)
            for z in range(2)
        ).astype(jnp.bfloat16)
        sorted_rows = jnp.dot(by_head, merged, preferred_element_type=jnp.float32).astype(
            jnp.bfloat16
        )
        for n in range(heads_each):
            values[s, me, :, n * VD : (n + 1) * VD] = jnp.dot(
                sorted_rows[n * half_tokens : (n + 1) * half_tokens],
                w_uv[n],
                preferred_element_type=jnp.float32,
            ).astype(jnp.bfloat16)
        hv_copies.append(
            [
                hand_on(s, me, lax.rem(my_chip + d, chips) * 2 + core, d)
                for d in range(1, chips)
            ]
        )
        passed.append([hand_on(s, me, sibling, chips)])

    out_copy.wait()
    depth = heads_each * VD

    def block(h):
        return jnp.dot(
            values[:, h].reshape(2 * half_tokens, depth),
            w_out[pl.ds(pl.multiple_of(h * depth, depth), depth)],
            preferred_element_type=jnp.float32,
        )

    result = block(me)
    for s in range(2):
        for d in range(1, chips):
            origin_chip = lax.rem(my_chip - d + chips, chips)
            hv_copies[s][d - 1].wait_recv()
            passed[s].append(hand_on(s, origin_chip * 2 + core, sibling, chips + d))
            if s == 1:
                result = result + block(origin_chip * 2 + core)
    for d in range(chips):
        for s in range(2):
            passed[s][d].wait_recv()
        result = result + block(lax.rem(my_chip - d + chips, chips) * 2 + 1 - core)
    out_ref[...] = result.astype(out_ref.dtype)

    for copies in mig_copies + kv_copies + lat_copies + hv_copies + passed + [q_copies]:
        for copy in copies:
            copy.wait_send()


def shards(old_pool, mig_source, mig_page, page_table, lengths, queries, new_latent, w_uv, w_out):
    groups = lax.axis_size("group")
    heads = lax.axis_size("head")
    own, rows, lat = old_pool.shape
    seqs, tokens, heads_each, _ = queries.shape
    migrate = mig_source.shape[1]
    slots = page_table.shape[1] // seqs
    features = w_out.shape[1]
    dims = (groups, heads, own, slots, rows, migrate, heads_each)
    columns = heads // 2
    width = slots * rows
    lines = tokens * heads_each
    spare = 128
    half = jnp.bfloat16
    anywhere = pl.BlockSpec(memory_space=pl.ANY)
    dma = pltpu.SemaphoreType.DMA
    count = len(CHUNKS)
    result = pl.pallas_call(
        functools.partial(kernel, dims, CHUNKS),
        out_shape=jax.ShapeDtypeStruct((seqs * tokens, features), half),
        in_specs=[anywhere] * 9,
        out_specs=pl.BlockSpec(memory_space=pltpu.VMEM),
        scratch_shapes=[
            pltpu.SMEM((groups, 1, migrate), jnp.int32),
            pltpu.SMEM((groups, migrate), jnp.int32),
            pltpu.SMEM(page_table.shape, jnp.int32),
            pltpu.SMEM(lengths.shape, jnp.int32),
            pltpu.SMEM((migrate,), jnp.int32),
            pltpu.VMEM(new_latent.shape, half),
            pltpu.VMEM((spare, lat), half),
            pltpu.VMEM((own, rows, lat), half),
            pltpu.VMEM((heads, 2, lines, lat), half),
            pltpu.VMEM((2, heads * lines, columns * width), jnp.float32),
            pltpu.VMEM((2, heads, lines, KVR + 128), half),
            pltpu.VMEM((2, heads, lines, KVR + 128), half),
            pltpu.VMEM((2, heads, columns * tokens, heads_each * VD), half),
            pltpu.VMEM(w_uv.shape, half),
            pltpu.VMEM(w_out.shape, half),
            [pltpu.VMEM((own + groups * CAP, rows, size), half) for _, size in CHUNKS],
            [pltpu.VMEM((groups, CAP, rows, size), half) for _, size in CHUNKS[:-1]]
            + [pltpu.VMEM((groups, rows, CAP * ROPE), half)],
            pltpu.VMEM((groups, rows, CAP * ROPE), half),
            [pltpu.VMEM((columns, 2 * width, size), half) for _, size in CHUNKS],
            [pltpu.VMEM((columns, 2 * width, size), half) for _, size in CHUNKS[:-1]]
            + [pltpu.VMEM((columns, width, 2 * ROPE), half)],
            pltpu.VMEM((columns, width, 2 * ROPE), half),
            dma((count, groups)),
            dma((count, groups)),
            dma((2, columns)),
            dma((2, columns)),
            dma((count, columns)),
            dma((count, columns)),
            dma((2, heads)),
            dma((2, heads)),
            dma((2, heads)),
            dma((2, heads)),
            dma((9 + count,)),
        ],
        compiler_params=pltpu.CompilerParams(
            collective_id=0, has_side_effects=True, vmem_limit_bytes=62 * 1024 * 1024
        ),
    )(
        jnp.transpose(mig_source, (0, 2, 1)),
        mig_page,
        page_table,
        lengths,
        old_pool,
        queries.reshape(2, columns, lines, lat),
        new_latent,
        w_uv,
        w_out,
    )
    return result.reshape(seqs, tokens, features)


def solution(mesh):
    return jax.shard_map(
        shards,
        mesh=mesh,
        in_specs=(
            P("group", "head", None),
            P(),
            P(),
            P("group", None),
            P("group"),
            P("group", None, "head", None),
            P("group", None, None),
            P("head", None, None),
            P(None, "head"),
        ),
        out_specs=P("group", None, "head"),
        check_vma=False,
    )
```

```python
import functools

import jax
import jax.numpy as jnp
from jax import lax
from jax.experimental import pallas as pl
from jax.experimental.pallas import tpu as pltpu
from jax.sharding import PartitionSpec as P

KVR = 512
ROPE = 64
VD = 128
CAP = 2
MESH = pl.DeviceIdType.MESH
HIDDEN = -1e30
PASS_AT = 2
CHUNKS = ((0, 128), (128, 128), (256, 128), (384, 128), (512, 64))


def kernel(
    dims,
    chunks,
    source_hbm,
    page_hbm,
    table_hbm,
    length_hbm,
    pool_hbm,
    query_hbm,
    new_hbm,
    w_uv_hbm,
    w_out_hbm,
    out_ref,
    source,
    page_of,
    table,
    length_of,
    place,
    new,
    new_keys,
    pool,
    queries,
    scores,
    lat_out,
    lat_in,
    values,
    w_uv,
    w_out,
    pages,
    mig_out,
    mig_in,
    keys,
    kv_out,
    kv_in,
    mig_send,
    mig_recv,
    q_send,
    q_recv,
    kv_send,
    kv_recv,
    lat_send,
    lat_recv,
    hv_send,
    hv_recv,
    local_sem,
):
    groups, heads, own, slots, rows, migrate, heads_each = dims
    my_group = lax.axis_index("group")
    me = lax.axis_index("head")
    columns = heads // 2
    part = lax.rem(me // 2, 2)
    column = me // 4 * 2 + lax.rem(me, 2)
    lat = pool_hbm.shape[2]
    width = slots * rows
    block_rows = 2 * width
    parts = range(len(chunks))
    last = len(chunks) - 1

    mine_at = part * columns + column

    def device_of(col, half):
        return col // 2 * 4 + half * 2 + lax.rem(col, 2)

    def place_of(head):
        return lax.rem(head // 2, 2) * columns + head // 4 * 2 + lax.rem(head, 2)

    def fetch(src, dst, n):
        copy = pltpu.make_async_copy(src, dst, local_sem.at[n])
        copy.start()
        return copy

    def remote(src, dst, send, recv, group, head):
        copy = pltpu.make_async_remote_copy(
            src_ref=src,
            dst_ref=dst,
            send_sem=send,
            recv_sem=recv,
            device_id=(group, head),
            device_id_type=MESH,
        )
        copy.start()
        return copy

    def settle(ref, sem):
        pltpu.make_async_copy(ref, ref, sem).wait()

    index_copies = [
        fetch(source_hbm, source, 0),
        fetch(page_hbm, page_of, 1),
        fetch(table_hbm, table, 2),
        fetch(length_hbm, length_of, 3),
    ]
    pool_copy = fetch(pool_hbm, pool, 4)
    barrier = pltpu.get_barrier_semaphore()
    for d in range(1, groups):
        to = lax.rem(my_group + d, groups)
        pl.semaphore_signal(barrier, inc=1, device_id=(to, me), device_id_type=MESH)
    for d in range(1, heads):
        to = lax.rem(me + d, heads)
        pl.semaphore_signal(barrier, inc=1, device_id=(my_group, to), device_id_type=MESH)

    new_copy = fetch(new_hbm, new, 5)
    query_copy = fetch(query_hbm.at[:, column], queries.at[mine_at], 6)
    page_copies = [
        fetch(
            pool_hbm.at[:, :, pl.ds(start, size)], pages[c].at[pl.ds(0, own)], 9 + c
        )
        for c, (start, size) in enumerate(chunks)
    ]
    uv_copy = fetch(w_uv_hbm, w_uv, 7)
    out_copy = fetch(w_out_hbm, w_out, 8)

    def wanted_by(group):
        first = jnp.int32(0)
        second = jnp.int32(0)
        for j in reversed(range(migrate)):
            mine = source[group, 0, j] == my_group
            second = jnp.where(mine, first, second)
            first = jnp.where(mine, page_of[group, j], first)
        return first, second

    for copy in index_copies:
        copy.wait()
    pool_copy.wait()
    group_order = sorted(range(1, groups), key=lambda d: -min(d, groups - d))
    picked = [wanted_by(lax.rem(my_group + d, groups)) for d in range(groups)]

    def gather(c):
        start, size = chunks[c]
        for d in range(groups):
            if c < last:
                for r, page in enumerate(picked[d]):
                    cut = pool[page, :, start : start + size]
                    if d == 0:
                        pages[c][own + my_group * CAP + r] = cut
                    else:
                        mig_out[c][d, r] = cut
            else:
                rotary = jnp.concatenate(
                    [pool[page, :, start : start + size] for page in picked[d]], axis=1
                )
                if d == 0:
                    mig_in[my_group] = rotary
                else:
                    mig_out[c][d] = rotary

    def send_migration(c):
        for d in group_order:
            remote(
                mig_out[c].at[d],
                pages[c].at[pl.ds(own + my_group * CAP, CAP)]
                if c < last
                else mig_in.at[my_group],
                mig_send.at[c],
                mig_recv.at[c],
                lax.rem(my_group + d, groups),
                me,
            )

    column_order = sorted(range(1, columns), key=lambda d: -min(d, columns - d))

    def send_queries():
        for d in column_order:
            col = lax.rem(column + d, columns)
            remote(
                query_hbm.at[:, col],
                queries.at[mine_at],
                q_send.at[0],
                q_recv.at[0],
                my_group,
                device_of(col, part),
            )

    def pass_queries():
        query_copy.wait()
        settle(queries.at[pl.ds(0, columns - 1)], q_recv.at[0])
        half = queries.at[pl.ds(pl.multiple_of(part * columns, columns), columns)]
        remote(half, half, q_send.at[1], q_recv.at[1], my_group, device_of(column, 1 - part))

    gather(0)
    pl.semaphore_wait(barrier, groups + heads - 2)
    send_migration(0)
    send_queries()
    for c in parts[1:]:
        gather(c)
        send_migration(c)

    for j in range(migrate):
        from_group = source[my_group, 0, j]
        rank = jnp.int32(0)
        for i in range(j):
            rank = rank + jnp.where(source[my_group, 0, i] == from_group, 1, 0)
        place[j] = own + from_group * CAP + rank

    new_copy.wait()
    spare = new_keys.shape[0]
    entry = lax.broadcasted_iota(jnp.int32, (spare, 2 * heads), 0)
    pick = (
        lax.broadcasted_iota(jnp.int32, (spare, 2 * heads), 1)
        == entry // 2 * heads + 2 * column + entry % 2
    ) & (entry < 4)
    new_keys[...] = jnp.dot(
        jnp.where(pick, 1.0, 0.0).astype(jnp.bfloat16),
        new[...].reshape(2 * heads, lat),
        preferred_element_type=jnp.float32,
    ).astype(jnp.bfloat16)

    def page_at(seq, k):
        page = table[0, seq * slots + k]
        return jnp.where(page < own, page, place[jnp.maximum(page - own, 0)])

    at = []
    for d in range(columns):
        col = lax.rem(column + d, columns)
        at.append([page_at(n // slots * columns + col, n % slots) for n in range(2 * slots)])

    for c in parts:
        page_copies[c].wait()
        settle(mig_out[c].at[pl.ds(1, groups - 1)], mig_recv.at[c])
        if c == last:
            for g in range(groups):
                for r in range(CAP):
                    pages[c][own + g * CAP + r] = mig_in[g, :, r * ROPE : (r + 1) * ROPE]

        def fill(block, d, c=c):
            if c < last:
                for n in range(2 * slots):
                    block[n * rows : (n + 1) * rows] = pages[c][at[d][n]]
                return
            for n in range(slots):
                k = n // 2 * slots + n % 2
                block[n * rows : (n + 1) * rows] = jnp.concatenate(
                    [pages[c][at[d][k]], pages[c][at[d][k + 2]]], axis=1
                )

        landing = keys[c] if c < last else kv_in
        for d in column_order:
            fill(kv_out[c].at[d], d)
            remote(
                kv_out[c].at[d],
                landing.at[column],
                kv_send.at[c],
                kv_recv.at[c],
                my_group,
                device_of(lax.rem(column + d, columns), part),
            )
        fill(landing.at[column], 0)
        if c == PASS_AT:
            pass_queries()

    for c in parts:
        settle(mig_out[c].at[pl.ds(1, groups - 1)], mig_send.at[c])

    row_count = heads * 2 * heads_each
    lanes = columns * width
    scale = (VD + ROPE) ** (-0.5)

    settle(queries.at[pl.ds(0, columns - 1)], q_send.at[0])
    settle(queries.at[pl.ds(0, columns)], q_send.at[1])
    settle(queries.at[pl.ds(0, columns)], q_recv.at[1])

    def dot_keys(s, start, size, key_rows):
        return lax.dot_general(
            queries[:, s, :, start : start + size].reshape(row_count, size),
            key_rows,
            (((1,), (1,)), ((), ())),
            preferred_element_type=jnp.float32,
        )

    def key_rows(c, s, size):
        return keys[c][:, s * width : (s + 1) * width, :size].reshape(lanes, size)

    for c, (start, size) in enumerate(chunks):
        settle(kv_out[c].at[pl.ds(1, columns - 1)], kv_recv.at[c])
        if c == last:
            for col in range(columns):
                for n in range(4):
                    keys[c][col, n * 2 * rows : (n + 1) * 2 * rows] = kv_in[
                        col,
                        n // 2 * 2 * rows : (n // 2 + 1) * 2 * rows,
                        n % 2 * ROPE : (n % 2 + 1) * ROPE,
                    ]
        for s in range(2):
            some = dot_keys(s, start, size, key_rows(c, s, size))
            scores[s] = some if c == 0 else scores[s] + some

    number = lax.broadcasted_iota(jnp.int32, (1, lanes), 1)
    from_column = number // width
    position = (
        number // rows % slots * (rows * heads)
        + device_of(from_column, part) * rows
        + number % rows
    )
    new_column = lax.broadcasted_iota(jnp.int32, (row_count, spare), 1)
    token = lax.broadcasted_iota(jnp.int32, (row_count, spare), 0) // heads_each % 2
    stat_lane = lax.broadcasted_iota(jnp.int32, (row_count, 128), 1)

    def in_three(value):
        out = []
        for _ in range(3):
            top = value.astype(jnp.bfloat16).astype(jnp.float32)
            out.append(top)
            value = value - top
        return out

    head_order = sorted(range(1, heads), key=lambda d: -min(d, heads - d))
    held = []
    stats = jnp.zeros((row_count, 128), jnp.float32)
    for s in range(2):
        new_shown = (
            (new_column >= 2 * s) & (new_column - 2 * s <= token) & (new_column < 2 * s + 2)
        ) & (part == 0)
        new_scores = jnp.where(
            new_shown, dot_keys(s, 0, lat, new_keys[...]) * scale, HIDDEN
        )
        shown = jnp.where(
            position < length_of[s * columns + column], scores[s] * scale, HIDDEN
        )
        highest = jnp.maximum(
            jnp.max(new_scores, axis=1, keepdims=True), jnp.max(shown, axis=1, keepdims=True)
        )
        new_weights = jnp.exp(new_scores - highest)
        weights = jnp.exp(shown - highest)
        totals = jnp.sum(new_weights, axis=1, keepdims=True) + jnp.sum(
            weights, axis=1, keepdims=True
        )
        for n, piece in enumerate(in_three(highest) + in_three(totals)):
            stats = jnp.where(stat_lane == 6 * s + n, piece, stats)
        held.append(
            (weights.astype(jnp.bfloat16), new_weights.astype(jnp.bfloat16), 1.0 / totals)
        )
    lat_out[0][:, :, KVR:] = stats.astype(jnp.bfloat16).reshape(heads, -1, 128)
    for s in range(2):
        weights, new_weights, share = held[s]
        for c, (start, size) in enumerate(chunks):
            size = min(size, KVR - start)
            if size > 0:
                weighted = jnp.dot(
                    weights, key_rows(c, s, size), preferred_element_type=jnp.float32
                ) + jnp.dot(
                    new_weights,
                    new_keys[:, start : start + size],
                    preferred_element_type=jnp.float32,
                )
                lat_out[s][:, :, start : start + size] = (
                    (weighted * share).astype(jnp.bfloat16).reshape(heads, -1, size)
                )
        for d in head_order:
            to = lax.rem(me + d, heads)
            remote(
                lat_out[s].at[place_of(to)],
                lat_in[s].at[mine_at],
                lat_send.at[s],
                lat_recv.at[s],
                my_group,
                to,
            )
        lat_in[s][mine_at] = lat_out[s][mine_at]
    for c in parts:
        settle(kv_out[c].at[pl.ds(1, columns - 1)], kv_send.at[c])

    half_tokens = 2 * columns
    half_rows = half_tokens * heads_each
    target = lax.broadcasted_iota(jnp.int32, (half_rows, half_rows), 0)
    origin = lax.broadcasted_iota(jnp.int32, (half_rows, half_rows), 1)
    by_head = jnp.where(
        origin == target % half_tokens * heads_each + target // half_tokens, 1.0, 0.0
    ).astype(jnp.bfloat16)

    chips = heads // 2
    my_chip, core = me // 2, lax.rem(me, 2)
    sibling = my_chip * 2 + 1 - core

    def hand_on(s, h, to, n):
        return remote(
            values.at[s, h],
            values.at[s, h],
            hv_send.at[s],
            hv_recv.at[s, n],
            my_group,
            to,
        )

    uv_copy.wait()
    hv_copies = []
    passed = []
    for s in range(2):
        settle(lat_out[s].at[pl.ds(0, heads - 1)], lat_recv.at[s])
        if s == 0:
            stat = []
            for z in range(2):
                tile = lat_in[0][z * columns : (z + 1) * columns, :, KVR:]
                stat.append(tile.reshape(half_rows, 128).astype(jnp.float32))

        def joined(z, n):
            return stat[z][:, n : n + 1] + stat[z][:, n + 1 : n + 2] + stat[z][:, n + 2 : n + 3]

        peaks = [joined(z, 6 * s) for z in range(2)]
        top = jnp.maximum(peaks[0], peaks[1])
        shares = [joined(z, 6 * s + 3) * jnp.exp(peaks[z] - top) for z in range(2)]
        whole = shares[0] + shares[1]
        merged = sum(
            lat_in[s][z * columns : (z + 1) * columns, :, :KVR]
            .reshape(half_rows, KVR)
            .astype(jnp.float32)
            * (shares[z] / whole)
            for z in range(2)
        ).astype(jnp.bfloat16)
        sorted_rows = jnp.dot(by_head, merged, preferred_element_type=jnp.float32).astype(
            jnp.bfloat16
        )
        for n in range(heads_each):
            values[s, me, :, n * VD : (n + 1) * VD] = jnp.dot(
                sorted_rows[n * half_tokens : (n + 1) * half_tokens],
                w_uv[n],
                preferred_element_type=jnp.float32,
            ).astype(jnp.bfloat16)
        hv_copies.append(
            [
                hand_on(s, me, lax.rem(my_chip + d, chips) * 2 + core, d)
                for d in range(1, chips)
            ]
        )
        passed.append([hand_on(s, me, sibling, chips)])

    for s in range(2):
        settle(lat_out[s].at[pl.ds(0, heads - 1)], lat_send.at[s])
    out_copy.wait()
    depth = heads_each * VD

    def block(h):
        return jnp.dot(
            values[:, h].reshape(2 * half_tokens, depth),
            w_out[pl.ds(pl.multiple_of(h * depth, depth), depth)],
            preferred_element_type=jnp.float32,
        )

    result = block(me)
    for s in range(2):
        for d in range(1, chips):
            origin_chip = lax.rem(my_chip - d + chips, chips)
            hv_copies[s][d - 1].wait_recv()
            passed[s].append(hand_on(s, origin_chip * 2 + core, sibling, chips + d))
            if s == 1:
                result = result + block(origin_chip * 2 + core)
    for d in range(chips):
        for s in range(2):
            passed[s][d].wait_recv()
        result = result + block(lax.rem(my_chip - d + chips, chips) * 2 + 1 - core)
    out_ref[...] = result.astype(out_ref.dtype)

    for s in range(2):
        settle(values.at[s, pl.ds(0, 2 * chips - 1)], hv_send.at[s])


def shards(old_pool, mig_source, mig_page, page_table, lengths, queries, new_latent, w_uv, w_out):
    groups = lax.axis_size("group")
    heads = lax.axis_size("head")
    own, rows, lat = old_pool.shape
    seqs, tokens, heads_each, _ = queries.shape
    migrate = mig_source.shape[1]
    slots = page_table.shape[1] // seqs
    features = w_out.shape[1]
    dims = (groups, heads, own, slots, rows, migrate, heads_each)
    columns = heads // 2
    width = slots * rows
    lines = tokens * heads_each
    spare = 128
    half = jnp.bfloat16
    anywhere = pl.BlockSpec(memory_space=pl.ANY)
    dma = pltpu.SemaphoreType.DMA
    count = len(CHUNKS)
    result = pl.pallas_call(
        functools.partial(kernel, dims, CHUNKS),
        out_shape=jax.ShapeDtypeStruct((seqs * tokens, features), half),
        in_specs=[anywhere] * 9,
        out_specs=pl.BlockSpec(memory_space=pltpu.VMEM),
        scratch_shapes=[
            pltpu.SMEM((groups, 1, migrate), jnp.int32),
            pltpu.SMEM((groups, migrate), jnp.int32),
            pltpu.SMEM(page_table.shape, jnp.int32),
            pltpu.SMEM(lengths.shape, jnp.int32),
            pltpu.SMEM((migrate,), jnp.int32),
            pltpu.VMEM(new_latent.shape, half),
            pltpu.VMEM((spare, lat), half),
            pltpu.VMEM((own, rows, lat), half),
            pltpu.VMEM((heads, 2, lines, lat), half),
            pltpu.VMEM((2, heads * lines, columns * width), jnp.float32),
            [pltpu.VMEM((heads, lines, size), half) for size in (KVR + 128, KVR)],
            [pltpu.VMEM((heads, lines, size), half) for size in (KVR + 128, KVR)],
            pltpu.VMEM((2, heads, columns * tokens, heads_each * VD), half),
            pltpu.VMEM(w_uv.shape, half),
            pltpu.VMEM(w_out.shape, half),
            [pltpu.VMEM((own + groups * CAP, rows, size), half) for _, size in CHUNKS],
            [pltpu.VMEM((groups, CAP, rows, size), half) for _, size in CHUNKS[:-1]]
            + [pltpu.VMEM((groups, rows, CAP * ROPE), half)],
            pltpu.VMEM((groups, rows, CAP * ROPE), half),
            [pltpu.VMEM((columns, 2 * width, size), half) for _, size in CHUNKS],
            [pltpu.VMEM((columns, 2 * width, size), half) for _, size in CHUNKS[:-1]]
            + [pltpu.VMEM((columns, width, 2 * ROPE), half)],
            pltpu.VMEM((columns, width, 2 * ROPE), half),
            dma((count,)),
            dma((count,)),
            dma((2,)),
            dma((2,)),
            dma((count,)),
            dma((count,)),
            dma((2,)),
            dma((2,)),
            dma((2,)),
            dma((2, heads)),
            dma((9 + count,)),
        ],
        compiler_params=pltpu.CompilerParams(
            collective_id=0, has_side_effects=True, vmem_limit_bytes=62 * 1024 * 1024
        ),
    )(
        jnp.transpose(mig_source, (0, 2, 1)),
        mig_page,
        page_table,
        lengths,
        old_pool,
        queries.reshape(2, columns, lines, lat),
        new_latent,
        w_uv,
        w_out,
    )
    return result.reshape(seqs, tokens, features)


def solution(mesh):
    return jax.shard_map(
        shards,
        mesh=mesh,
        in_specs=(
            P("group", "head", None),
            P(),
            P(),
            P("group", None),
            P("group"),
            P("group", None, "head", None),
            P("group", None, None),
            P("head", None, None),
            P(None, "head"),
        ),
        out_specs=P("group", None, "head"),
        check_vma=False,
    )
```

```python
import functools

import jax
import jax.numpy as jnp
from jax import lax
from jax.experimental import pallas as pl
from jax.experimental.pallas import tpu as pltpu
from jax.sharding import PartitionSpec as P

KVR = 512
ROPE = 64
VD = 128
CAP = 2
MESH = pl.DeviceIdType.MESH
HIDDEN = -1e30
PASS_AT = 2
CHUNKS = ((0, 128), (128, 128), (256, 128), (384, 128), (512, 64))


def kernel(
    dims,
    chunks,
    source_hbm,
    page_hbm,
    table_hbm,
    length_hbm,
    pool_hbm,
    query_hbm,
    new_hbm,
    w_uv_hbm,
    w_out_hbm,
    out_ref,
    source,
    page_of,
    table,
    length_of,
    place,
    new,
    new_keys,
    pool,
    q_raw,
    q_out,
    queries,
    scores,
    lat_out,
    lat_in,
    values,
    w_uv,
    w_out,
    pages,
    mig_out,
    mig_in,
    keys,
    kv_out,
    kv_in,
    mig_send,
    mig_recv,
    q_send,
    q_recv,
    kv_send,
    kv_recv,
    lat_send,
    lat_recv,
    hv_send,
    hv_recv,
    local_sem,
):
    groups, heads, own, slots, rows, migrate, heads_each = dims
    my_group = lax.axis_index("group")
    me = lax.axis_index("head")
    columns = heads // 2
    part = lax.rem(me // 2, 2)
    column = me // 4 * 2 + lax.rem(me, 2)
    lat = pool_hbm.shape[2]
    width = slots * rows
    block_rows = 2 * width
    parts = range(len(chunks))
    last = len(chunks) - 1

    mine_at = part * columns + column

    def device_of(col, half):
        return col // 2 * 4 + half * 2 + lax.rem(col, 2)

    def fetch(src, dst, n):
        copy = pltpu.make_async_copy(src, dst, local_sem.at[n])
        copy.start()
        return copy

    def remote(src, dst, send, recv, group, head):
        copy = pltpu.make_async_remote_copy(
            src_ref=src,
            dst_ref=dst,
            send_sem=send,
            recv_sem=recv,
            device_id=(group, head),
            device_id_type=MESH,
        )
        copy.start()
        return copy

    def settle(ref, sem):
        pltpu.make_async_copy(ref, ref, sem).wait()

    index_copies = [
        fetch(source_hbm, source, 0),
        fetch(page_hbm, page_of, 1),
        fetch(table_hbm, table, 2),
        fetch(length_hbm, length_of, 3),
    ]
    pool_copy = fetch(pool_hbm, pool, 4)
    barrier = pltpu.get_barrier_semaphore()
    for d in range(1, groups):
        to = lax.rem(my_group + d, groups)
        pl.semaphore_signal(barrier, inc=1, device_id=(to, me), device_id_type=MESH)
    for d in range(1, heads):
        to = lax.rem(me + d, heads)
        pl.semaphore_signal(barrier, inc=1, device_id=(my_group, to), device_id_type=MESH)

    new_copy = fetch(new_hbm, new, 5)
    query_copy = fetch(query_hbm, q_raw, 6)
    page_copies = [
        fetch(
            pool_hbm.at[:, :, pl.ds(start, size)], pages[c].at[pl.ds(0, own)], 9 + c
        )
        for c, (start, size) in enumerate(chunks)
    ]
    uv_copy = fetch(w_uv_hbm, w_uv, 7)
    out_copy = fetch(w_out_hbm, w_out, 8)

    def wanted_by(group):
        first = jnp.int32(0)
        second = jnp.int32(0)
        for j in reversed(range(migrate)):
            mine = source[group, 0, j] == my_group
            second = jnp.where(mine, first, second)
            first = jnp.where(mine, page_of[group, j], first)
        return first, second

    for copy in index_copies:
        copy.wait()
    pool_copy.wait()
    group_order = sorted(range(1, groups), key=lambda d: -min(d, groups - d))
    picked = [wanted_by(lax.rem(my_group + d, groups)) for d in range(groups)]

    def gather(c):
        start, size = chunks[c]
        for d in range(groups):
            if c < last:
                for r, page in enumerate(picked[d]):
                    cut = pool[page, :, start : start + size]
                    if d == 0:
                        pages[c][own + my_group * CAP + r] = cut
                    else:
                        mig_out[c][d, r] = cut
            else:
                rotary = jnp.concatenate(
                    [pool[page, :, start : start + size] for page in picked[d]], axis=1
                )
                if d == 0:
                    mig_in[my_group] = rotary
                else:
                    mig_out[c][d] = rotary

    def send_migration(c):
        for d in group_order:
            remote(
                mig_out[c].at[d],
                pages[c].at[pl.ds(own + my_group * CAP, CAP)]
                if c < last
                else mig_in.at[my_group],
                mig_send.at[c],
                mig_recv.at[c],
                lax.rem(my_group + d, groups),
                me,
            )

    column_order = sorted(range(1, columns), key=lambda d: -min(d, columns - d))

    def send_queries():
        query_copy.wait()
        for col in range(columns):
            for s in range(2):
                q_out[col, :, s * KVR : (s + 1) * KVR] = q_raw[s, col, :, :KVR]
            q_out[col, :, 2 * KVR :] = jnp.concatenate(
                [q_raw[s, col, :, KVR:] for s in range(2)], axis=1
            )
        queries[mine_at] = q_out[column]
        for d in column_order:
            col = lax.rem(column + d, columns)
            remote(
                q_out.at[col],
                queries.at[mine_at],
                q_send.at[0],
                q_recv.at[0],
                my_group,
                device_of(col, part),
            )

    def pass_queries():
        settle(queries.at[pl.ds(0, columns - 1)], q_recv.at[0])
        half = queries.at[pl.ds(pl.multiple_of(part * columns, columns), columns)]
        remote(half, half, q_send.at[1], q_recv.at[1], my_group, device_of(column, 1 - part))

    gather(0)
    pl.semaphore_wait(barrier, groups + heads - 2)
    send_migration(0)
    send_queries()
    for c in parts[1:]:
        gather(c)
        send_migration(c)

    for j in range(migrate):
        from_group = source[my_group, 0, j]
        rank = jnp.int32(0)
        for i in range(j):
            rank = rank + jnp.where(source[my_group, 0, i] == from_group, 1, 0)
        place[j] = own + from_group * CAP + rank

    new_copy.wait()
    spare = new_keys.shape[0]
    entry = lax.broadcasted_iota(jnp.int32, (spare, 2 * heads), 0)
    pick = (
        lax.broadcasted_iota(jnp.int32, (spare, 2 * heads), 1)
        == entry // 2 * heads + 2 * column + entry % 2
    ) & (entry < 4)
    new_keys[...] = jnp.dot(
        jnp.where(pick, 1.0, 0.0).astype(jnp.bfloat16),
        new[...].reshape(2 * heads, lat),
        preferred_element_type=jnp.float32,
    ).astype(jnp.bfloat16)

    def page_at(seq, k):
        page = table[0, seq * slots + k]
        return jnp.where(page < own, page, place[jnp.maximum(page - own, 0)])

    at = []
    for d in range(columns):
        col = lax.rem(column + d, columns)
        at.append([page_at(n // slots * columns + col, n % slots) for n in range(2 * slots)])

    for c in parts:
        page_copies[c].wait()
        settle(mig_out[c].at[pl.ds(1, groups - 1)], mig_recv.at[c])
        if c == last:
            for g in range(groups):
                for r in range(CAP):
                    pages[c][own + g * CAP + r] = mig_in[g, :, r * ROPE : (r + 1) * ROPE]

        def fill(block, d, c=c):
            if c < last:
                for n in range(2 * slots):
                    block[n * rows : (n + 1) * rows] = pages[c][at[d][n]]
                return
            for n in range(slots):
                k = n // 2 * slots + n % 2
                block[n * rows : (n + 1) * rows] = jnp.concatenate(
                    [pages[c][at[d][k]], pages[c][at[d][k + 2]]], axis=1
                )

        landing = keys[c] if c < last else kv_in
        for d in column_order:
            fill(kv_out[c].at[d], d)
            remote(
                kv_out[c].at[d],
                landing.at[column],
                kv_send.at[c],
                kv_recv.at[c],
                my_group,
                device_of(lax.rem(column + d, columns), part),
            )
        fill(landing.at[column], 0)
        if c == PASS_AT:
            pass_queries()

    for c in parts:
        settle(mig_out[c].at[pl.ds(1, groups - 1)], mig_send.at[c])

    row_count = heads * 2 * heads_each
    lanes = columns * width
    scale = (VD + ROPE) ** (-0.5)

    settle(queries.at[pl.ds(0, columns - 1)], q_send.at[0])
    settle(queries.at[pl.ds(0, columns)], q_send.at[1])
    settle(queries.at[pl.ds(0, columns)], q_recv.at[1])

    def dot_keys(s, start, size, key_rows):
        first = s * KVR + start if start < KVR else 2 * KVR + s * ROPE
        return lax.dot_general(
            queries[:, :, first : first + size].reshape(row_count, size),
            key_rows,
            (((1,), (1,)), ((), ())),
            preferred_element_type=jnp.float32,
        )

    def key_rows(c, s, size):
        return keys[c][:, s * width : (s + 1) * width, :size].reshape(lanes, size)

    for c, (start, size) in enumerate(chunks):
        settle(kv_out[c].at[pl.ds(1, columns - 1)], kv_recv.at[c])
        if c == last:
            for col in range(columns):
                for n in range(4):
                    keys[c][col, n * 2 * rows : (n + 1) * 2 * rows] = kv_in[
                        col,
                        n // 2 * 2 * rows : (n // 2 + 1) * 2 * rows,
                        n % 2 * ROPE : (n % 2 + 1) * ROPE,
                    ]
        for s in range(2):
            some = dot_keys(s, start, size, key_rows(c, s, size))
            scores[s] = some if c == 0 else scores[s] + some

    number = lax.broadcasted_iota(jnp.int32, (1, lanes), 1)
    from_column = number // width
    position = (
        number // rows % slots * (rows * heads)
        + device_of(from_column, part) * rows
        + number % rows
    )
    new_column = lax.broadcasted_iota(jnp.int32, (row_count, spare), 1)
    token = lax.broadcasted_iota(jnp.int32, (row_count, spare), 0) // heads_each % 2
    stat_lane = lax.broadcasted_iota(jnp.int32, (row_count, 128), 1)

    def in_three(value):
        out = []
        for _ in range(3):
            top = value.astype(jnp.bfloat16).astype(jnp.float32)
            out.append(top)
            value = value - top
        return out

    held = []
    stats = jnp.zeros((row_count, 128), jnp.float32)
    for s in range(2):
        new_shown = (
            (new_column >= 2 * s) & (new_column - 2 * s <= token) & (new_column < 2 * s + 2)
        ) & (part == 0)
        new_scores = jnp.where(
            new_shown,
            (
                dot_keys(s, 0, KVR, new_keys[:, :KVR])
                + dot_keys(s, KVR, ROPE, new_keys[:, KVR:])
            )
            * scale,
            HIDDEN,
        )
        shown = jnp.where(
            position < length_of[s * columns + column], scores[s] * scale, HIDDEN
        )
        highest = jnp.maximum(
            jnp.max(new_scores, axis=1, keepdims=True), jnp.max(shown, axis=1, keepdims=True)
        )
        new_weights = jnp.exp(new_scores - highest)
        weights = jnp.exp(shown - highest)
        totals = jnp.sum(new_weights, axis=1, keepdims=True) + jnp.sum(
            weights, axis=1, keepdims=True
        )
        for n, piece in enumerate(in_three(highest) + in_three(totals)):
            stats = jnp.where(stat_lane == 6 * s + n, piece, stats)
        held.append(
            (weights.astype(jnp.bfloat16), new_weights.astype(jnp.bfloat16), 1.0 / totals)
        )
    lat_out[0][:, :, KVR:] = stats.astype(jnp.bfloat16).reshape(heads, -1, 128)
    for s in range(2):
        weights, new_weights, share = held[s]
        for c, (start, size) in enumerate(chunks):
            size = min(size, KVR - start)
            if size > 0:
                weighted = jnp.dot(
                    weights, key_rows(c, s, size), preferred_element_type=jnp.float32
                ) + jnp.dot(
                    new_weights,
                    new_keys[:, start : start + size],
                    preferred_element_type=jnp.float32,
                )
                lat_out[s][:, :, start : start + size] = (
                    (weighted * share).astype(jnp.bfloat16).reshape(heads, -1, size)
                )
        for cross in (True, False):
            half = 1 - part if cross else part
            for d in column_order + [0] * cross:
                col = lax.rem(column + d, columns)
                remote(
                    lat_out[s].at[half * columns + col],
                    lat_in[s].at[mine_at],
                    lat_send.at[s],
                    lat_recv.at[s],
                    my_group,
                    device_of(col, half),
                )
        lat_in[s][mine_at] = lat_out[s][mine_at]
    for c in parts:
        settle(kv_out[c].at[pl.ds(1, columns - 1)], kv_send.at[c])

    half_tokens = 2 * columns
    half_rows = half_tokens * heads_each
    target = lax.broadcasted_iota(jnp.int32, (half_rows, half_rows), 0)
    origin = lax.broadcasted_iota(jnp.int32, (half_rows, half_rows), 1)
    by_head = jnp.where(
        origin == target % half_tokens * heads_each + target // half_tokens, 1.0, 0.0
    ).astype(jnp.bfloat16)

    chips = heads // 2
    my_chip, core = me // 2, lax.rem(me, 2)
    sibling = my_chip * 2 + 1 - core

    def hand_on(s, h, to, n):
        return remote(
            values.at[s, h],
            values.at[s, h],
            hv_send.at[s],
            hv_recv.at[s, n],
            my_group,
            to,
        )

    uv_copy.wait()
    hv_copies = []
    passed = []
    for s in range(2):
        settle(lat_out[s].at[pl.ds(0, heads - 1)], lat_recv.at[s])
        if s == 0:
            stat = []
            for z in range(2):
                tile = lat_in[0][z * columns : (z + 1) * columns, :, KVR:]
                stat.append(tile.reshape(half_rows, 128).astype(jnp.float32))

        def joined(z, n):
            return stat[z][:, n : n + 1] + stat[z][:, n + 1 : n + 2] + stat[z][:, n + 2 : n + 3]

        peaks = [joined(z, 6 * s) for z in range(2)]
        top = jnp.maximum(peaks[0], peaks[1])
        shares = [joined(z, 6 * s + 3) * jnp.exp(peaks[z] - top) for z in range(2)]
        whole = shares[0] + shares[1]
        merged = sum(
            lat_in[s][z * columns : (z + 1) * columns, :, :KVR]
            .reshape(half_rows, KVR)
            .astype(jnp.float32)
            * (shares[z] / whole)
            for z in range(2)
        ).astype(jnp.bfloat16)
        sorted_rows = jnp.dot(by_head, merged, preferred_element_type=jnp.float32).astype(
            jnp.bfloat16
        )
        for n in range(heads_each):
            values[s, me, :, n * VD : (n + 1) * VD] = jnp.dot(
                sorted_rows[n * half_tokens : (n + 1) * half_tokens],
                w_uv[n],
                preferred_element_type=jnp.float32,
            ).astype(jnp.bfloat16)
        hv_copies.append(
            [
                hand_on(s, me, lax.rem(my_chip + d, chips) * 2 + core, d)
                for d in range(1, chips)
            ]
        )
        passed.append([hand_on(s, me, sibling, chips)])

    for s in range(2):
        settle(lat_out[s].at[pl.ds(0, heads - 1)], lat_send.at[s])
    out_copy.wait()
    depth = heads_each * VD

    def block(h):
        return jnp.dot(
            values[:, h].reshape(2 * half_tokens, depth),
            w_out[pl.ds(pl.multiple_of(h * depth, depth), depth)],
            preferred_element_type=jnp.float32,
        )

    result = block(me)
    for s in range(2):
        for d in range(1, chips):
            origin_chip = lax.rem(my_chip - d + chips, chips)
            hv_copies[s][d - 1].wait_recv()
            passed[s].append(hand_on(s, origin_chip * 2 + core, sibling, chips + d))
            if s == 1:
                result = result + block(origin_chip * 2 + core)
    for d in range(chips):
        for s in range(2):
            passed[s][d].wait_recv()
        result = result + block(lax.rem(my_chip - d + chips, chips) * 2 + 1 - core)
    out_ref[...] = result.astype(out_ref.dtype)

    for s in range(2):
        settle(values.at[s, pl.ds(0, 2 * chips - 1)], hv_send.at[s])


def shards(old_pool, mig_source, mig_page, page_table, lengths, queries, new_latent, w_uv, w_out):
    groups = lax.axis_size("group")
    heads = lax.axis_size("head")
    own, rows, lat = old_pool.shape
    seqs, tokens, heads_each, _ = queries.shape
    migrate = mig_source.shape[1]
    slots = page_table.shape[1] // seqs
    features = w_out.shape[1]
    dims = (groups, heads, own, slots, rows, migrate, heads_each)
    columns = heads // 2
    width = slots * rows
    lines = tokens * heads_each
    spare = 128
    half = jnp.bfloat16
    anywhere = pl.BlockSpec(memory_space=pltpu.HBM)
    dma = pltpu.SemaphoreType.DMA
    count = len(CHUNKS)
    result = pl.pallas_call(
        functools.partial(kernel, dims, CHUNKS),
        out_shape=jax.ShapeDtypeStruct((seqs * tokens, features), half),
        in_specs=[anywhere] * 9,
        out_specs=pl.BlockSpec(memory_space=pltpu.VMEM),
        scratch_shapes=[
            pltpu.SMEM((groups, 1, migrate), jnp.int32),
            pltpu.SMEM((groups, migrate), jnp.int32),
            pltpu.SMEM(page_table.shape, jnp.int32),
            pltpu.SMEM(lengths.shape, jnp.int32),
            pltpu.SMEM((migrate,), jnp.int32),
            pltpu.VMEM(new_latent.shape, half),
            pltpu.VMEM((spare, lat), half),
            pltpu.VMEM((own, rows, lat), half),
            pltpu.VMEM((2, columns, lines, lat), half),
            pltpu.VMEM((columns, lines, 2 * lat), half),
            pltpu.VMEM((heads, lines, 2 * lat), half),
            pltpu.VMEM((2, heads * lines, columns * width), jnp.float32),
            [pltpu.VMEM((heads, lines, size), half) for size in (KVR + 128, KVR)],
            [pltpu.VMEM((heads, lines, size), half) for size in (KVR + 128, KVR)],
            pltpu.VMEM((2, heads, columns * tokens, heads_each * VD), half),
            pltpu.VMEM(w_uv.shape, half),
            pltpu.VMEM(w_out.shape, half),
            [pltpu.VMEM((own + groups * CAP, rows, size), half) for _, size in CHUNKS],
            [pltpu.VMEM((groups, CAP, rows, size), half) for _, size in CHUNKS[:-1]]
            + [pltpu.VMEM((groups, rows, CAP * ROPE), half)],
            pltpu.VMEM((groups, rows, CAP * ROPE), half),
            [pltpu.VMEM((columns, 2 * width, size), half) for _, size in CHUNKS],
            [pltpu.VMEM((columns, 2 * width, size), half) for _, size in CHUNKS[:-1]]
            + [pltpu.VMEM((columns, width, 2 * ROPE), half)],
            pltpu.VMEM((columns, width, 2 * ROPE), half),
            dma((count,)),
            dma((count,)),
            dma((2,)),
            dma((2,)),
            dma((count,)),
            dma((count,)),
            dma((2,)),
            dma((2,)),
            dma((2,)),
            dma((2, heads)),
            dma((9 + count,)),
        ],
        compiler_params=pltpu.CompilerParams(
            collective_id=0, has_side_effects=True, vmem_limit_bytes=48 * 1024 * 1024
        ),
    )(
        *(
            pltpu.with_memory_space_constraint(operand, pltpu.HBM)
            for operand in (
                jnp.transpose(mig_source, (0, 2, 1)),
                mig_page,
                page_table,
                lengths,
                old_pool,
                queries.reshape(2, columns, lines, lat),
                new_latent,
                w_uv,
                w_out,
            )
        )
    )
    return result.reshape(seqs, tokens, features)


def solution(mesh):
    return jax.shard_map(
        shards,
        mesh=mesh,
        in_specs=(
            P("group", "head", None),
            P(),
            P(),
            P("group", None),
            P("group"),
            P("group", None, "head", None),
            P("group", None, None),
            P("head", None, None),
            P(None, "head"),
        ),
        out_specs=P("group", None, "head"),
        check_vma=False,
    )
```

```python
import functools

import jax
import jax.numpy as jnp
from jax import lax
from jax.experimental import pallas as pl
from jax.experimental.pallas import tpu as pltpu
from jax.sharding import PartitionSpec as P

KVR = 512
ROPE = 64
VD = 128
CAP = 2
MESH = pl.DeviceIdType.MESH
HIDDEN = -1e30
PASS_AT = 1
CHUNKS = ((0, 384), (384, 128), (512, 64))


def kernel(
    dims,
    chunks,
    source_hbm,
    page_hbm,
    table_hbm,
    length_hbm,
    pool_hbm,
    query_hbm,
    new_hbm,
    w_uv_hbm,
    w_out_hbm,
    out_ref,
    source,
    page_of,
    table,
    length_of,
    place,
    order,
    new,
    new_keys,
    pool,
    q_raw,
    q_out,
    queries,
    lat_out,
    lat_in,
    values,
    w_uv,
    w_out,
    pages,
    mig_out,
    mig_in,
    keys,
    rotary_in,
    rotary_keys,
    seq_keys,
    seq_rotary,
    own_out,
    own_rotary,
    kv_out,
    mig_send,
    mig_recv,
    q_send,
    q_recv,
    own_send,
    own_recv,
    kv_send,
    kv_recv,
    lat_send,
    lat_recv,
    hv_send,
    hv_recv,
    local_sem,
):
    groups, heads, own, slots, rows, migrate, heads_each = dims
    my_group = lax.axis_index("group")
    me = lax.axis_index("head")
    columns = heads // 2
    part = lax.rem(me // 2, 2)
    column = me // 4 * 2 + lax.rem(me, 2)
    lat = pool_hbm.shape[2]
    width = slots * rows
    early = slots
    parts = range(len(chunks))
    last = len(chunks) - 1

    mine_at = part * columns + column

    def device_of(col, half):
        return col // 2 * 4 + half * 2 + lax.rem(col, 2)

    def fetch(src, dst, n):
        copy = pltpu.make_async_copy(src, dst, local_sem.at[n])
        copy.start()
        return copy

    def remote(src, dst, send, recv, group, head):
        copy = pltpu.make_async_remote_copy(
            src_ref=src,
            dst_ref=dst,
            send_sem=send,
            recv_sem=recv,
            device_id=(group, head),
            device_id_type=MESH,
        )
        copy.start()
        return copy

    def settle(ref, sem):
        pltpu.make_async_copy(ref, ref, sem).wait()

    index_copies = [
        fetch(source_hbm, source, 0),
        fetch(page_hbm, page_of, 1),
        fetch(table_hbm, table, 2),
        fetch(length_hbm, length_of, 3),
    ]
    pool_copy = fetch(pool_hbm, pool, 4)
    barrier = pltpu.get_barrier_semaphore()
    for d in range(1, groups):
        to = lax.rem(my_group + d, groups)
        pl.semaphore_signal(barrier, inc=1, device_id=(to, me), device_id_type=MESH)
    for d in range(1, heads):
        to = lax.rem(me + d, heads)
        pl.semaphore_signal(barrier, inc=1, device_id=(my_group, to), device_id_type=MESH)

    new_copy = fetch(new_hbm, new, 5)
    query_copy = fetch(query_hbm, q_raw, 6)
    page_copies = [
        fetch(
            pool_hbm.at[:, :, pl.ds(start, size)], pages[c].at[pl.ds(0, own)], 9 + c
        )
        for c, (start, size) in enumerate(chunks)
    ]
    uv_copy = fetch(w_uv_hbm, w_uv, 7)
    out_copy = fetch(w_out_hbm, w_out, 8)

    def wanted_by(group):
        first = jnp.int32(0)
        second = jnp.int32(0)
        for j in reversed(range(migrate)):
            mine = source[group, 0, j] == my_group
            second = jnp.where(mine, first, second)
            first = jnp.where(mine, page_of[group, j], first)
        return first, second

    for copy in index_copies:
        copy.wait()
    pool_copy.wait()
    group_order = sorted(range(1, groups), key=lambda d: -min(d, groups - d))
    picked = [wanted_by(lax.rem(my_group + d, groups)) for d in range(groups)]

    def gather(c):
        start, size = chunks[c]
        for d in range(groups):
            if c < last:
                for r, page in enumerate(picked[d]):
                    cut = pool[page, :, start : start + size]
                    if d == 0:
                        pages[c][own + my_group * CAP + r] = cut
                    else:
                        mig_out[c][d, r] = cut
            else:
                rotary = jnp.concatenate(
                    [pool[page, :, start : start + size] for page in picked[d]], axis=1
                )
                if d == 0:
                    mig_in[my_group] = rotary
                else:
                    mig_out[c][d] = rotary

    def send_migration(c):
        for d in group_order:
            remote(
                mig_out[c].at[d],
                pages[c].at[pl.ds(own + my_group * CAP, CAP)]
                if c < last
                else mig_in.at[my_group],
                mig_send.at[c],
                mig_recv.at[c],
                lax.rem(my_group + d, groups),
                me,
            )

    column_order = sorted(range(1, columns), key=lambda d: -min(d, columns - d))

    def send_queries():
        query_copy.wait()
        for col in range(columns):
            pair = [q_raw[order[col]], q_raw[order[heads - 1 - col]]]
            for s in range(2):
                q_out[col, :, s * KVR : (s + 1) * KVR] = pair[s][:, :KVR]
            q_out[col, :, 2 * KVR :] = jnp.concatenate([one[:, KVR:] for one in pair], axis=1)
        queries[mine_at] = q_out[column]
        for d in column_order:
            col = lax.rem(column + d, columns)
            remote(
                q_out.at[col],
                queries.at[mine_at],
                q_send.at[0],
                q_recv.at[0],
                my_group,
                device_of(col, part),
            )

    def pass_queries():
        settle(queries.at[pl.ds(0, columns - 1)], q_recv.at[0])
        half = queries.at[pl.ds(pl.multiple_of(part * columns, columns), columns)]
        remote(half, half, q_send.at[1], q_recv.at[1], my_group, device_of(column, 1 - part))

    gather(0)
    pl.semaphore_wait(barrier, groups + heads - 2)
    send_migration(0)
    gather(1)
    send_migration(1)

    for j in range(migrate):
        from_group = source[my_group, 0, j]
        rank = jnp.int32(0)
        for i in range(j):
            rank = rank + jnp.where(source[my_group, 0, i] == from_group, 1, 0)
        place[j] = own + from_group * CAP + rank

    load = []
    for i in range(heads):
        moved = jnp.int32(0)
        for k in range(slots):
            moved = moved + jnp.where(table[0, i * slots + k] >= own, heads, 0)
        load.append(moved - i)
    ranks = [jnp.int32(0)] * heads
    for i in range(heads):
        for j in range(i):
            ahead = jnp.where(load[j] > load[i], 1, 0)
            ranks[i] = ranks[i] + ahead
            ranks[j] = ranks[j] + 1 - ahead
    for n in range(heads):
        found = jnp.int32(0)
        for i in range(heads):
            found = found + jnp.where(ranks[i] == n, i, 0)
        order[n] = found

    at = []
    home = []
    for d in range(columns):
        col = lax.rem(column + d, columns)
        pair = (order[col], order[heads - 1 - col])
        pages_of = [table[0, pair[n // slots] * slots + n % slots] for n in range(2 * slots)]
        stays = [jnp.where(page < own, 1, 0) for page in pages_of]
        behind = sum(stays)
        ahead = jnp.int32(0)
        spots = []
        for n in range(2 * slots):
            spots.append(jnp.where(pages_of[n] < own, ahead, behind + n - ahead))
            ahead = ahead + stays[n]
        if d == 0:
            home = spots
        wanted = [
            jnp.where(page < own, page, place[jnp.maximum(page - own, 0)]) for page in pages_of
        ]
        at.append(
            [
                sum(jnp.where(spots[n] == p, wanted[n], 0) for n in range(2 * slots))
                for p in range(2 * slots)
            ]
        )

    def send_own():
        for d in column_order + [0]:
            cut = [pool[jnp.minimum(at[d][p], own - 1)] for p in range(early)]
            pairs = [
                jnp.concatenate([cut[i][:, KVR:], cut[i + 2][:, KVR:]], axis=1) for i in range(2)
            ]
            for p in range(early):
                if d == 0:
                    keys[column, p] = cut[p][:, :KVR]
                else:
                    own_out[d, p] = cut[p][:, :KVR]
            for i in range(2):
                if d == 0:
                    rotary_in[0, column, i] = pairs[i]
                else:
                    own_rotary[d, i] = pairs[i]
            if d > 0:
                to = device_of(lax.rem(column + d, columns), part)
                remote(
                    own_out.at[d],
                    keys.at[column, pl.ds(0, early)],
                    own_send.at[0],
                    own_recv.at[0],
                    my_group,
                    to,
                )
                remote(
                    own_rotary.at[d],
                    rotary_in.at[0, column],
                    own_send.at[1],
                    own_recv.at[1],
                    my_group,
                    to,
                )

    send_own()
    for c in parts[2:]:
        gather(c)
        send_migration(c)
        if c == 2:
            send_queries()

    new_copy.wait()
    spare = new_keys.shape[0]
    entry = lax.broadcasted_iota(jnp.int32, (spare, 2 * heads), 0)
    line = lax.broadcasted_iota(jnp.int32, (spare, 2 * heads), 1)
    pick = (
        line
        == jnp.where(
            entry < 2, 2 * order[column] + entry, 2 * order[heads - 1 - column] + entry - 2
        )
    ) & (entry < 4)
    new_keys[...] = jnp.dot(
        jnp.where(pick, 1.0, 0.0).astype(jnp.bfloat16),
        new[...].reshape(2 * heads, lat),
        preferred_element_type=jnp.float32,
    ).astype(jnp.bfloat16)

    for c, (start, size) in enumerate(chunks):
        page_copies[c].wait()
        settle(mig_out[c].at[pl.ds(1, groups - 1)], mig_recv.at[c])
        if c == last:
            for g in range(groups):
                for r in range(CAP):
                    pages[c][own + g * CAP + r] = mig_in[g, :, r * ROPE : (r + 1) * ROPE]
        for d in column_order + [0]:
            cut = [pages[c][at[d][early + p]] for p in range(early)]
            if c == last:
                cut = [jnp.concatenate([cut[i], cut[i + 2]], axis=1) for i in range(2)]
            for p, value in enumerate(cut):
                if d > 0:
                    kv_out[c][d, p] = value
                elif c < last:
                    keys[column, early + p, :, start : start + size] = value
                else:
                    rotary_in[1, column, p] = value
            if d > 0:
                remote(
                    kv_out[c].at[d],
                    keys.at[column, pl.ds(early, early), :, pl.ds(start, size)]
                    if c < last
                    else rotary_in.at[1, column],
                    kv_send.at[c],
                    kv_recv.at[c],
                    my_group,
                    device_of(lax.rem(column + d, columns), part),
                )
        if c == PASS_AT:
            pass_queries()

    for c in parts:
        settle(mig_out[c].at[pl.ds(1, groups - 1)], mig_send.at[c])
    settle(own_out.at[pl.ds(1, columns - 1)], own_send.at[0])
    settle(own_rotary.at[pl.ds(1, columns - 1)], own_send.at[1])

    row_count = heads * 2 * heads_each
    lanes = columns * width
    scale = (VD + ROPE) ** (-0.5)

    settle(queries.at[pl.ds(0, columns - 1)], q_send.at[0])
    settle(queries.at[pl.ds(0, columns)], q_send.at[1])
    settle(queries.at[pl.ds(0, columns)], q_recv.at[1])

    def dot_keys(s, start, size, key_rows):
        first = s * KVR + start if start < KVR else 2 * KVR + s * ROPE
        return lax.dot_general(
            queries[:, :, first : first + size].reshape(row_count, size),
            key_rows,
            (((1,), (1,)), ((), ())),
            preferred_element_type=jnp.float32,
        )

    settle(own_out.at[pl.ds(1, columns - 1)], own_recv.at[0])
    settle(own_rotary.at[pl.ds(1, columns - 1)], own_recv.at[1])
    for c in parts:
        settle(kv_out[c].at[pl.ds(1, columns - 1)], kv_recv.at[c])
    for e in range(2):
        for i in range(2):
            rotary_keys[:, e * early + 2 * i : e * early + 2 * i + 2] = rotary_in[
                e, :, :, :, i * ROPE : (i + 1) * ROPE
            ]
    page_lanes = columns * rows
    for n in range(2 * slots):
        s, k = n // slots, n % slots
        here = pl.ds(k * page_lanes, page_lanes)
        seq_keys[s, here] = keys[:, home[n]].reshape(page_lanes, KVR)
        seq_rotary[s, here] = rotary_keys[:, home[n]].reshape(page_lanes, ROPE)

    number = lax.broadcasted_iota(jnp.int32, (1, lanes), 1)
    position = (
        number // page_lanes * (rows * heads)
        + device_of(number // rows % columns, part) * rows
        + number % rows
    )
    new_column = lax.broadcasted_iota(jnp.int32, (row_count, spare), 1)
    token = lax.broadcasted_iota(jnp.int32, (row_count, spare), 0) // heads_each % 2
    stat_lane = lax.broadcasted_iota(jnp.int32, (row_count, 128), 1)

    def in_three(value):
        out = []
        for _ in range(3):
            top = value.astype(jnp.bfloat16).astype(jnp.float32)
            out.append(top)
            value = value - top
        return out

    held = []
    stats = jnp.zeros((row_count, 128), jnp.float32)
    for s in range(2):
        new_shown = (
            (new_column >= 2 * s) & (new_column - 2 * s <= token) & (new_column < 2 * s + 2)
        ) & (part == 0)
        new_scores = jnp.where(
            new_shown,
            (
                dot_keys(s, 0, KVR, new_keys[:, :KVR])
                + dot_keys(s, KVR, ROPE, new_keys[:, KVR:])
            )
            * scale,
            HIDDEN,
        )
        shown = jnp.where(
            position < length_of[order[column if s == 0 else heads - 1 - column]],
            (dot_keys(s, 0, KVR, seq_keys[s]) + dot_keys(s, KVR, ROPE, seq_rotary[s])) * scale,
            HIDDEN,
        )
        highest = jnp.maximum(
            jnp.max(new_scores, axis=1, keepdims=True), jnp.max(shown, axis=1, keepdims=True)
        )
        new_weights = jnp.exp(new_scores - highest)
        weights = jnp.exp(shown - highest)
        totals = jnp.sum(new_weights, axis=1, keepdims=True) + jnp.sum(
            weights, axis=1, keepdims=True
        )
        for n, piece in enumerate(in_three(highest) + in_three(totals)):
            stats = jnp.where(stat_lane == 6 * s + n, piece, stats)
        held.append(
            (weights.astype(jnp.bfloat16), new_weights.astype(jnp.bfloat16), 1.0 / totals)
        )
    lat_out[0][:, :, KVR:] = stats.astype(jnp.bfloat16).reshape(heads, -1, 128)
    for s in range(2):
        weights, new_weights, share = held[s]
        for start in range(0, KVR, 256):
            span = slice(start, start + 256)
            weighted = jnp.dot(
                weights, seq_keys[s, :, span], preferred_element_type=jnp.float32
            ) + jnp.dot(new_weights, new_keys[:, span], preferred_element_type=jnp.float32)
            lat_out[s][:, :, span] = (
                (weighted * share).astype(jnp.bfloat16).reshape(heads, -1, 256)
            )
        for cross in (True, False):
            half = 1 - part if cross else part
            for d in column_order + [0] * cross:
                col = lax.rem(column + d, columns)
                remote(
                    lat_out[s].at[half * columns + col],
                    lat_in[s].at[mine_at],
                    lat_send.at[s],
                    lat_recv.at[s],
                    my_group,
                    device_of(col, half),
                )
        lat_in[s][mine_at] = lat_out[s][mine_at]
    for c in parts:
        settle(kv_out[c].at[pl.ds(1, columns - 1)], kv_send.at[c])

    half_tokens = 2 * columns
    half_rows = half_tokens * heads_each
    target = lax.broadcasted_iota(jnp.int32, (half_rows, half_rows), 0)
    origin = lax.broadcasted_iota(jnp.int32, (half_rows, half_rows), 1)
    by_head = jnp.where(
        origin == target % half_tokens * heads_each + target // half_tokens, 1.0, 0.0
    ).astype(jnp.bfloat16)

    seat = lax.broadcasted_iota(jnp.int32, (2 * heads, 2 * heads), 1)
    row = seat % 2
    for n in range(heads):
        seq = order[n if n < columns else heads - 1 - (n - columns)]
        row = row + jnp.where(seat // 2 == n, 2 * seq, 0)
    by_sequence = jnp.where(
        lax.broadcasted_iota(jnp.int32, (2 * heads, 2 * heads), 0) == row, 1.0, 0.0
    ).astype(jnp.bfloat16)

    chips = heads // 2
    my_chip, core = me // 2, lax.rem(me, 2)
    sibling = my_chip * 2 + 1 - core
    chip_order = sorted(range(1, chips), key=lambda d: -min(d, chips - d))

    def hand_on(s, h, to, n):
        return remote(
            values.at[s, h],
            values.at[s, h],
            hv_send.at[s],
            hv_recv.at[s, n],
            my_group,
            to,
        )

    uv_copy.wait()
    hv_copies = []
    passed = []
    for s in range(2):
        settle(lat_out[s].at[pl.ds(0, heads - 1)], lat_recv.at[s])
        if s == 0:
            stat = []
            for z in range(2):
                tile = lat_in[0][z * columns : (z + 1) * columns, :, KVR:]
                stat.append(tile.reshape(half_rows, 128).astype(jnp.float32))

        def joined(z, n):
            return stat[z][:, n : n + 1] + stat[z][:, n + 1 : n + 2] + stat[z][:, n + 2 : n + 3]

        peaks = [joined(z, 6 * s) for z in range(2)]
        top = jnp.maximum(peaks[0], peaks[1])
        shares = [joined(z, 6 * s + 3) * jnp.exp(peaks[z] - top) for z in range(2)]
        whole = shares[0] + shares[1]
        merged = sum(
            lat_in[s][z * columns : (z + 1) * columns, :, :KVR]
            .reshape(half_rows, KVR)
            .astype(jnp.float32)
            * (shares[z] / whole)
            for z in range(2)
        ).astype(jnp.bfloat16)
        sorted_rows = jnp.dot(by_head, merged, preferred_element_type=jnp.float32).astype(
            jnp.bfloat16
        )
        for n in range(heads_each):
            values[s, me, :, n * VD : (n + 1) * VD] = jnp.dot(
                sorted_rows[n * half_tokens : (n + 1) * half_tokens],
                w_uv[n],
                preferred_element_type=jnp.float32,
            ).astype(jnp.bfloat16)
        hv_copies.append(
            [
                hand_on(s, me, lax.rem(my_chip + d, chips) * 2 + core, d)
                for d in chip_order
            ]
        )
        passed.append([hand_on(s, me, sibling, chips)])

    for s in range(2):
        settle(lat_out[s].at[pl.ds(0, heads - 1)], lat_send.at[s])
    out_copy.wait()
    depth = heads_each * VD

    def block(h):
        return jnp.dot(
            values[:, h].reshape(2 * half_tokens, depth),
            w_out[pl.ds(pl.multiple_of(h * depth, depth), depth)],
            preferred_element_type=jnp.float32,
        )

    result = block(me)
    for s in range(2):
        for n, d in enumerate(chip_order):
            origin_chip = lax.rem(my_chip - d + chips, chips)
            hv_copies[s][n].wait_recv()
            passed[s].append(hand_on(s, origin_chip * 2 + core, sibling, chips + d))
            if s == 1:
                result = result + block(origin_chip * 2 + core)
    for k, d in enumerate([0] + chip_order):
        for s in range(2):
            passed[s][k].wait_recv()
        result = result + block(lax.rem(my_chip - d + chips, chips) * 2 + 1 - core)
    out_ref[...] = jnp.dot(
        by_sequence, result.astype(jnp.bfloat16), preferred_element_type=jnp.float32
    ).astype(out_ref.dtype)

    for s in range(2):
        settle(values.at[s, pl.ds(0, 2 * chips - 1)], hv_send.at[s])


def shards(old_pool, mig_source, mig_page, page_table, lengths, queries, new_latent, w_uv, w_out):
    groups = lax.axis_size("group")
    heads = lax.axis_size("head")
    own, rows, lat = old_pool.shape
    seqs, tokens, heads_each, _ = queries.shape
    migrate = mig_source.shape[1]
    slots = page_table.shape[1] // seqs
    features = w_out.shape[1]
    dims = (groups, heads, own, slots, rows, migrate, heads_each)
    columns = heads // 2
    width = slots * rows
    lines = tokens * heads_each
    spare = 128
    half = jnp.bfloat16
    anywhere = pl.BlockSpec(memory_space=pltpu.HBM)
    dma = pltpu.SemaphoreType.DMA
    count = len(CHUNKS)
    result = pl.pallas_call(
        functools.partial(kernel, dims, CHUNKS),
        out_shape=jax.ShapeDtypeStruct((seqs * tokens, features), half),
        in_specs=[anywhere] * 9,
        out_specs=pl.BlockSpec(memory_space=pltpu.VMEM),
        scratch_shapes=[
            pltpu.SMEM((groups, 1, migrate), jnp.int32),
            pltpu.SMEM((groups, migrate), jnp.int32),
            pltpu.SMEM(page_table.shape, jnp.int32),
            pltpu.SMEM(lengths.shape, jnp.int32),
            pltpu.SMEM((migrate,), jnp.int32),
            pltpu.SMEM((heads,), jnp.int32),
            pltpu.VMEM(new_latent.shape, half),
            pltpu.VMEM((spare, lat), half),
            pltpu.VMEM((own, rows, lat), half),
            pltpu.VMEM((seqs, lines, lat), half),
            pltpu.VMEM((columns, lines, 2 * lat), half),
            pltpu.VMEM((heads, lines, 2 * lat), half),
            [pltpu.VMEM((heads, lines, size), half) for size in (KVR + 128, KVR)],
            [pltpu.VMEM((heads, lines, size), half) for size in (KVR + 128, KVR)],
            pltpu.VMEM((2, heads, columns * tokens, heads_each * VD), half),
            pltpu.VMEM(w_uv.shape, half),
            pltpu.VMEM(w_out.shape, half),
            [pltpu.VMEM((own + groups * CAP, rows, size), half) for _, size in CHUNKS],
            [pltpu.VMEM((groups, CAP, rows, size), half) for _, size in CHUNKS[:-1]]
            + [pltpu.VMEM((groups, rows, CAP * ROPE), half)],
            pltpu.VMEM((groups, rows, CAP * ROPE), half),
            pltpu.VMEM((columns, 2 * slots, rows, KVR), half),
            pltpu.VMEM((2, columns, 2, rows, 2 * ROPE), half),
            pltpu.VMEM((columns, 2 * slots, rows, ROPE), half),
            pltpu.VMEM((2, columns * width, KVR), half),
            pltpu.VMEM((2, columns * width, ROPE), half),
            pltpu.VMEM((columns, slots, rows, KVR), half),
            pltpu.VMEM((columns, 2, rows, 2 * ROPE), half),
            [pltpu.VMEM((columns, slots, rows, size), half) for _, size in CHUNKS[:-1]]
            + [pltpu.VMEM((columns, 2, rows, 2 * ROPE), half)],
            dma((count,)),
            dma((count,)),
            dma((2,)),
            dma((2,)),
            dma((2,)),
            dma((2,)),
            dma((count,)),
            dma((count,)),
            dma((2,)),
            dma((2,)),
            dma((2,)),
            dma((2, heads)),
            dma((9 + count,)),
        ],
        compiler_params=pltpu.CompilerParams(
            collective_id=0, has_side_effects=True, vmem_limit_bytes=48 * 1024 * 1024
        ),
    )(
        *(
            pltpu.with_memory_space_constraint(operand, pltpu.HBM)
            for operand in (
                jnp.transpose(mig_source, (0, 2, 1)),
                mig_page,
                page_table,
                lengths,
                old_pool,
                queries.reshape(seqs, lines, lat),
                new_latent,
                w_uv,
                w_out,
            )
        )
    )
    return result.reshape(seqs, tokens, features)


def solution(mesh):
    return jax.shard_map(
        shards,
        mesh=mesh,
        in_specs=(
            P("group", "head", None),
            P(),
            P(),
            P("group", None),
            P("group"),
            P("group", None, "head", None),
            P("group", None, None),
            P("head", None, None),
            P(None, "head"),
        ),
        out_specs=P("group", None, "head"),
        check_vma=False,
    )
```

```python
import functools

import jax
import jax.numpy as jnp
from jax import lax
from jax.experimental import pallas as pl
from jax.experimental.pallas import tpu as pltpu
from jax.sharding import PartitionSpec as P

KVR = 512
ROPE = 64
VD = 128
CAP = 2
MESH = pl.DeviceIdType.MESH
HIDDEN = -1e30
PASS_AT = 0
CHUNKS = ((0, 384), (384, 128), (512, 64))


def kernel(
    dims,
    chunks,
    source_hbm,
    page_hbm,
    table_hbm,
    length_hbm,
    pool_hbm,
    query_hbm,
    new_hbm,
    w_uv_hbm,
    w_out_hbm,
    out_ref,
    source,
    page_of,
    table,
    length_of,
    place,
    order,
    new,
    new_keys,
    pool,
    q_raw,
    q_out,
    queries,
    lat_out,
    lat_in,
    values,
    w_uv,
    w_out,
    pages,
    mig_out,
    mig_in,
    keys,
    rotary_in,
    rotary_keys,
    seq_keys,
    seq_rotary,
    own_out,
    own_rotary,
    kv_out,
    mig_send,
    mig_recv,
    q_send,
    q_recv,
    own_send,
    own_recv,
    kv_send,
    kv_recv,
    lat_send,
    lat_recv,
    hv_send,
    hv_recv,
    local_sem,
):
    groups, heads, own, slots, rows, migrate, heads_each = dims
    my_group = lax.axis_index("group")
    me = lax.axis_index("head")
    columns = heads // 2
    part = lax.rem(me // 2, 2)
    column = me // 4 * 2 + lax.rem(me, 2)
    lat = pool_hbm.shape[2]
    width = slots * rows
    early = slots
    parts = range(len(chunks))
    last = len(chunks) - 1

    mine_at = part * columns + column

    def device_of(col, half):
        return col // 2 * 4 + half * 2 + lax.rem(col, 2)

    def fetch(src, dst, n):
        copy = pltpu.make_async_copy(src, dst, local_sem.at[n])
        copy.start()
        return copy

    def remote(src, dst, send, recv, group, head):
        copy = pltpu.make_async_remote_copy(
            src_ref=src,
            dst_ref=dst,
            send_sem=send,
            recv_sem=recv,
            device_id=(group, head),
            device_id_type=MESH,
        )
        copy.start()
        return copy

    def settle(ref, sem):
        pltpu.make_async_copy(ref, ref, sem).wait()

    group_order = sorted(range(1, groups), key=lambda d: -min(d, groups - d))
    barrier = pltpu.get_barrier_semaphore()
    for d in group_order:
        to = lax.rem(my_group + d, groups)
        pl.semaphore_signal(barrier, inc=1, device_id=(to, me), device_id_type=MESH)
    for d in sorted(range(1, heads), key=lambda d: -min(d, heads - d)):
        to = lax.rem(me + d, heads)
        pl.semaphore_signal(barrier, inc=1, device_id=(my_group, to), device_id_type=MESH)

    index_copies = [
        fetch(source_hbm, source, 0),
        fetch(page_hbm, page_of, 1),
        fetch(table_hbm, table, 2),
        fetch(length_hbm, length_of, 3),
    ]
    pool_copy = fetch(pool_hbm, pool, 4)
    new_copy = fetch(new_hbm, new, 5)
    query_copy = fetch(query_hbm, q_raw, 6)
    page_copies = [
        fetch(
            pool_hbm.at[:, :, pl.ds(start, size)], pages[c].at[pl.ds(0, own)], 9 + c
        )
        for c, (start, size) in enumerate(chunks)
    ]
    uv_copy = fetch(w_uv_hbm, w_uv, 7)
    out_copy = fetch(w_out_hbm, w_out, 8)

    def wanted_by(group):
        first = jnp.int32(0)
        second = jnp.int32(0)
        for j in reversed(range(migrate)):
            mine = source[group, 0, j] == my_group
            second = jnp.where(mine, first, second)
            first = jnp.where(mine, page_of[group, j], first)
        return first, second

    for copy in index_copies:
        copy.wait()
    pool_copy.wait()
    picked = [wanted_by(lax.rem(my_group + d, groups)) for d in range(groups)]

    def gather(c):
        start, size = chunks[c]
        for d in range(groups):
            if c < last:
                for r, page in enumerate(picked[d]):
                    cut = pool[page, :, start : start + size]
                    if d == 0:
                        pages[c][own + my_group * CAP + r] = cut
                    else:
                        mig_out[c][d, r] = cut
            else:
                rotary = jnp.concatenate(
                    [pool[page, :, start : start + size] for page in picked[d]], axis=1
                )
                if d == 0:
                    mig_in[my_group] = rotary
                else:
                    mig_out[c][d] = rotary

    def send_migration(c):
        for d in group_order:
            remote(
                mig_out[c].at[d],
                pages[c].at[pl.ds(own + my_group * CAP, CAP)]
                if c < last
                else mig_in.at[my_group],
                mig_send.at[c],
                mig_recv.at[c],
                lax.rem(my_group + d, groups),
                me,
            )

    column_order = sorted(range(1, columns), key=lambda d: -min(d, columns - d))

    def send_queries():
        query_copy.wait()
        for col in range(columns):
            pair = [q_raw[order[col]], q_raw[order[heads - 1 - col]]]
            for s in range(2):
                q_out[col, :, s * KVR : (s + 1) * KVR] = pair[s][:, :KVR]
            q_out[col, :, 2 * KVR :] = jnp.concatenate([one[:, KVR:] for one in pair], axis=1)
        queries[mine_at] = q_out[column]
        for d in column_order:
            col = lax.rem(column + d, columns)
            remote(
                q_out.at[col],
                queries.at[mine_at],
                q_send.at[0],
                q_recv.at[0],
                my_group,
                device_of(col, part),
            )

    def pass_queries():
        settle(queries.at[pl.ds(0, columns - 1)], q_recv.at[0])
        half = queries.at[pl.ds(pl.multiple_of(part * columns, columns), columns)]
        remote(half, half, q_send.at[1], q_recv.at[1], my_group, device_of(column, 1 - part))

    gather(0)
    pl.semaphore_wait(barrier, groups + heads - 2)
    send_migration(0)
    gather(1)
    send_migration(1)

    for j in range(migrate):
        from_group = source[my_group, 0, j]
        rank = jnp.int32(0)
        for i in range(j):
            rank = rank + jnp.where(source[my_group, 0, i] == from_group, 1, 0)
        place[j] = own + from_group * CAP + rank

    load = []
    for i in range(heads):
        moved = jnp.int32(0)
        for k in range(slots):
            moved = moved + jnp.where(table[0, i * slots + k] >= own, heads, 0)
        load.append(moved - i)
    ranks = [jnp.int32(0)] * heads
    for i in range(heads):
        for j in range(i):
            ahead = jnp.where(load[j] > load[i], 1, 0)
            ranks[i] = ranks[i] + ahead
            ranks[j] = ranks[j] + 1 - ahead
    for n in range(heads):
        found = jnp.int32(0)
        for i in range(heads):
            found = found + jnp.where(ranks[i] == n, i, 0)
        order[n] = found

    at = []
    home = []
    for d in range(columns):
        col = lax.rem(column + d, columns)
        pair = (order[col], order[heads - 1 - col])
        pages_of = [table[0, pair[n // slots] * slots + n % slots] for n in range(2 * slots)]
        stays = [jnp.where(page < own, 1, 0) for page in pages_of]
        behind = sum(stays)
        ahead = jnp.int32(0)
        spots = []
        for n in range(2 * slots):
            spots.append(jnp.where(pages_of[n] < own, ahead, behind + n - ahead))
            ahead = ahead + stays[n]
        if d == 0:
            home = spots
        wanted = [
            jnp.where(page < own, page, place[jnp.maximum(page - own, 0)]) for page in pages_of
        ]
        at.append(
            [
                sum(jnp.where(spots[n] == p, wanted[n], 0) for n in range(2 * slots))
                for p in range(2 * slots)
            ]
        )

    def send_own():
        for d in column_order + [0]:
            cut = [pool[jnp.minimum(at[d][p], own - 1)] for p in range(early)]
            pairs = [
                jnp.concatenate([cut[i][:, KVR:], cut[i + 2][:, KVR:]], axis=1) for i in range(2)
            ]
            for p in range(early):
                if d == 0:
                    keys[column, p] = cut[p][:, :KVR]
                else:
                    own_out[d, p] = cut[p][:, :KVR]
            for i in range(2):
                if d == 0:
                    rotary_in[0, column, i] = pairs[i]
                else:
                    own_rotary[d, i] = pairs[i]
            if d > 0:
                to = device_of(lax.rem(column + d, columns), part)
                remote(
                    own_out.at[d],
                    keys.at[column, pl.ds(0, early)],
                    own_send.at[0],
                    own_recv.at[0],
                    my_group,
                    to,
                )
                remote(
                    own_rotary.at[d],
                    rotary_in.at[0, column],
                    own_send.at[1],
                    own_recv.at[1],
                    my_group,
                    to,
                )

    send_own()
    for c in parts[2:]:
        gather(c)
        send_migration(c)
        if c == 2:
            send_queries()

    new_copy.wait()
    spare = new_keys.shape[0]
    entry = lax.broadcasted_iota(jnp.int32, (spare, 2 * heads), 0)
    line = lax.broadcasted_iota(jnp.int32, (spare, 2 * heads), 1)
    pick = (
        line
        == jnp.where(
            entry < 2, 2 * order[column] + entry, 2 * order[heads - 1 - column] + entry - 2
        )
    ) & (entry < 4)
    new_keys[...] = jnp.dot(
        jnp.where(pick, 1.0, 0.0).astype(jnp.bfloat16),
        new[...].reshape(2 * heads, lat),
        preferred_element_type=jnp.float32,
    ).astype(jnp.bfloat16)

    for c, (start, size) in enumerate(chunks):
        page_copies[c].wait()
        settle(mig_out[c].at[pl.ds(1, groups - 1)], mig_recv.at[c])
        if c == last:
            for g in range(groups):
                for r in range(CAP):
                    pages[c][own + g * CAP + r] = mig_in[g, :, r * ROPE : (r + 1) * ROPE]
        for d in column_order + [0]:
            cut = [pages[c][at[d][early + p]] for p in range(early)]
            if c == last:
                cut = [jnp.concatenate([cut[i], cut[i + 2]], axis=1) for i in range(2)]
            for p, value in enumerate(cut):
                if d > 0:
                    kv_out[c][d, p] = value
                elif c < last:
                    keys[column, early + p, :, start : start + size] = value
                else:
                    rotary_in[1, column, p] = value
            if d > 0:
                remote(
                    kv_out[c].at[d],
                    keys.at[column, pl.ds(early, early), :, pl.ds(start, size)]
                    if c < last
                    else rotary_in.at[1, column],
                    kv_send.at[c],
                    kv_recv.at[c],
                    my_group,
                    device_of(lax.rem(column + d, columns), part),
                )
        if c == PASS_AT:
            pass_queries()

    for c in parts:
        settle(mig_out[c].at[pl.ds(1, groups - 1)], mig_send.at[c])
    settle(own_out.at[pl.ds(1, columns - 1)], own_send.at[0])
    settle(own_rotary.at[pl.ds(1, columns - 1)], own_send.at[1])

    row_count = heads * 2 * heads_each
    lanes = columns * width
    scale = (VD + ROPE) ** (-0.5)

    settle(queries.at[pl.ds(0, columns - 1)], q_send.at[0])
    settle(queries.at[pl.ds(0, columns)], q_send.at[1])
    settle(queries.at[pl.ds(0, columns)], q_recv.at[1])

    def dot_keys(s, start, size, key_rows):
        first = s * KVR + start if start < KVR else 2 * KVR + s * ROPE
        return lax.dot_general(
            queries[:, :, first : first + size].reshape(row_count, size),
            key_rows,
            (((1,), (1,)), ((), ())),
            preferred_element_type=jnp.float32,
        )

    settle(own_out.at[pl.ds(1, columns - 1)], own_recv.at[0])
    settle(own_rotary.at[pl.ds(1, columns - 1)], own_recv.at[1])
    for c in parts:
        settle(kv_out[c].at[pl.ds(1, columns - 1)], kv_recv.at[c])
    for e in range(2):
        for i in range(2):
            rotary_keys[:, e * early + 2 * i : e * early + 2 * i + 2] = rotary_in[
                e, :, :, :, i * ROPE : (i + 1) * ROPE
            ]
    page_lanes = columns * rows
    for n in range(2 * slots):
        s, k = n // slots, n % slots
        here = pl.ds(k * page_lanes, page_lanes)
        seq_keys[s, here] = keys[:, home[n]].reshape(page_lanes, KVR)
        seq_rotary[s, here] = rotary_keys[:, home[n]].reshape(page_lanes, ROPE)

    number = lax.broadcasted_iota(jnp.int32, (1, lanes), 1)
    position = (
        number // page_lanes * (rows * heads)
        + device_of(number // rows % columns, part) * rows
        + number % rows
    )
    new_column = lax.broadcasted_iota(jnp.int32, (row_count, spare), 1)
    token = lax.broadcasted_iota(jnp.int32, (row_count, spare), 0) // heads_each % 2
    stat_lane = lax.broadcasted_iota(jnp.int32, (row_count, 128), 1)

    def in_three(value):
        out = []
        for _ in range(3):
            top = value.astype(jnp.bfloat16).astype(jnp.float32)
            out.append(top)
            value = value - top
        return out

    held = []
    stats = jnp.zeros((row_count, 128), jnp.float32)
    for s in range(2):
        new_shown = (
            (new_column >= 2 * s) & (new_column - 2 * s <= token) & (new_column < 2 * s + 2)
        ) & (part == 0)
        new_scores = jnp.where(
            new_shown,
            (
                dot_keys(s, 0, KVR, new_keys[:, :KVR])
                + dot_keys(s, KVR, ROPE, new_keys[:, KVR:])
            )
            * scale,
            HIDDEN,
        )
        shown = jnp.where(
            position < length_of[order[column if s == 0 else heads - 1 - column]],
            (dot_keys(s, 0, KVR, seq_keys[s]) + dot_keys(s, KVR, ROPE, seq_rotary[s])) * scale,
            HIDDEN,
        )
        highest = jnp.maximum(
            jnp.max(new_scores, axis=1, keepdims=True), jnp.max(shown, axis=1, keepdims=True)
        )
        new_weights = jnp.exp(new_scores - highest)
        weights = jnp.exp(shown - highest)
        totals = jnp.sum(new_weights, axis=1, keepdims=True) + jnp.sum(
            weights, axis=1, keepdims=True
        )
        for n, piece in enumerate(in_three(highest) + in_three(totals)):
            stats = jnp.where(stat_lane == 6 * s + n, piece, stats)
        held.append(
            (weights.astype(jnp.bfloat16), new_weights.astype(jnp.bfloat16), 1.0 / totals)
        )
    lat_out[0][:, :, KVR:] = stats.astype(jnp.bfloat16).reshape(heads, -1, 128)
    for s in range(2):
        weights, new_weights, share = held[s]
        for start in range(0, KVR, 256):
            span = slice(start, start + 256)
            weighted = jnp.dot(
                weights, seq_keys[s, :, span], preferred_element_type=jnp.float32
            ) + jnp.dot(new_weights, new_keys[:, span], preferred_element_type=jnp.float32)
            lat_out[s][:, :, span] = (
                (weighted * share).astype(jnp.bfloat16).reshape(heads, -1, 256)
            )
        for cross in (False, True):
            half = 1 - part if cross else part
            for d in column_order + [0] * cross:
                col = lax.rem(column + d, columns)
                remote(
                    lat_out[s].at[half * columns + col],
                    lat_in[s].at[mine_at],
                    lat_send.at[s],
                    lat_recv.at[s],
                    my_group,
                    device_of(col, half),
                )
        lat_in[s][mine_at] = lat_out[s][mine_at]
    for c in parts:
        settle(kv_out[c].at[pl.ds(1, columns - 1)], kv_send.at[c])

    half_tokens = 2 * columns
    half_rows = half_tokens * heads_each
    target = lax.broadcasted_iota(jnp.int32, (half_rows, half_rows), 0)
    origin = lax.broadcasted_iota(jnp.int32, (half_rows, half_rows), 1)
    by_head = jnp.where(
        origin == target % half_tokens * heads_each + target // half_tokens, 1.0, 0.0
    ).astype(jnp.bfloat16)

    seat = lax.broadcasted_iota(jnp.int32, (2 * heads, 2 * heads), 1)
    row = seat % 2
    for n in range(heads):
        seq = order[n if n < columns else heads - 1 - (n - columns)]
        row = row + jnp.where(seat // 2 == n, 2 * seq, 0)
    by_sequence = jnp.where(
        lax.broadcasted_iota(jnp.int32, (2 * heads, 2 * heads), 0) == row, 1.0, 0.0
    ).astype(jnp.bfloat16)

    chips = heads // 2
    my_chip, core = me // 2, lax.rem(me, 2)
    sibling = my_chip * 2 + 1 - core
    chip_order = sorted(range(1, chips), key=lambda d: -min(d, chips - d))

    def hand_on(s, h, to, n):
        return remote(
            values.at[s, h],
            values.at[s, h],
            hv_send.at[s],
            hv_recv.at[s, n],
            my_group,
            to,
        )

    uv_copy.wait()
    hv_copies = []
    passed = []
    for s in range(2):
        settle(lat_out[s].at[pl.ds(0, heads - 1)], lat_recv.at[s])
        if s == 0:
            stat = []
            for z in range(2):
                tile = lat_in[0][z * columns : (z + 1) * columns, :, KVR:]
                stat.append(tile.reshape(half_rows, 128).astype(jnp.float32))

        def joined(z, n):
            return stat[z][:, n : n + 1] + stat[z][:, n + 1 : n + 2] + stat[z][:, n + 2 : n + 3]

        peaks = [joined(z, 6 * s) for z in range(2)]
        top = jnp.maximum(peaks[0], peaks[1])
        shares = [joined(z, 6 * s + 3) * jnp.exp(peaks[z] - top) for z in range(2)]
        whole = shares[0] + shares[1]
        merged = sum(
            lat_in[s][z * columns : (z + 1) * columns, :, :KVR]
            .reshape(half_rows, KVR)
            .astype(jnp.float32)
            * (shares[z] / whole)
            for z in range(2)
        ).astype(jnp.bfloat16)
        sorted_rows = jnp.dot(by_head, merged, preferred_element_type=jnp.float32).astype(
            jnp.bfloat16
        )
        for n in range(heads_each):
            values[s, me, :, n * VD : (n + 1) * VD] = jnp.dot(
                sorted_rows[n * half_tokens : (n + 1) * half_tokens],
                w_uv[n],
                preferred_element_type=jnp.float32,
            ).astype(jnp.bfloat16)
        hv_copies.append(
            [
                hand_on(s, me, lax.rem(my_chip + d, chips) * 2 + core, d)
                for d in chip_order
            ]
        )
        passed.append([hand_on(s, me, sibling, chips)])

    for s in range(2):
        settle(lat_out[s].at[pl.ds(0, heads - 1)], lat_send.at[s])
    out_copy.wait()
    depth = heads_each * VD

    def block(h):
        return jnp.dot(
            values[:, h].reshape(2 * half_tokens, depth),
            w_out[pl.ds(pl.multiple_of(h * depth, depth), depth)],
            preferred_element_type=jnp.float32,
        )

    result = block(me)
    for s in range(2):
        for n, d in enumerate(chip_order):
            origin_chip = lax.rem(my_chip - d + chips, chips)
            hv_copies[s][n].wait_recv()
            passed[s].append(hand_on(s, origin_chip * 2 + core, sibling, chips + d))
            if s == 1:
                result = result + block(origin_chip * 2 + core)
    for k, d in enumerate([0] + chip_order):
        for s in range(2):
            passed[s][k].wait_recv()
        result = result + block(lax.rem(my_chip - d + chips, chips) * 2 + 1 - core)
    out_ref[...] = jnp.dot(
        by_sequence, result.astype(jnp.bfloat16), preferred_element_type=jnp.float32
    ).astype(out_ref.dtype)

    for s in range(2):
        settle(values.at[s, pl.ds(0, 2 * chips - 1)], hv_send.at[s])


def shards(old_pool, mig_source, mig_page, page_table, lengths, queries, new_latent, w_uv, w_out):
    groups = lax.axis_size("group")
    heads = lax.axis_size("head")
    own, rows, lat = old_pool.shape
    seqs, tokens, heads_each, _ = queries.shape
    migrate = mig_source.shape[1]
    slots = page_table.shape[1] // seqs
    features = w_out.shape[1]
    dims = (groups, heads, own, slots, rows, migrate, heads_each)
    columns = heads // 2
    width = slots * rows
    lines = tokens * heads_each
    spare = 128
    half = jnp.bfloat16
    anywhere = pl.BlockSpec(memory_space=pltpu.HBM)
    dma = pltpu.SemaphoreType.DMA
    count = len(CHUNKS)
    result = pl.pallas_call(
        functools.partial(kernel, dims, CHUNKS),
        out_shape=jax.ShapeDtypeStruct((seqs * tokens, features), half),
        in_specs=[anywhere] * 9,
        out_specs=pl.BlockSpec(memory_space=pltpu.VMEM),
        scratch_shapes=[
            pltpu.SMEM((groups, 1, migrate), jnp.int32),
            pltpu.SMEM((groups, migrate), jnp.int32),
            pltpu.SMEM(page_table.shape, jnp.int32),
            pltpu.SMEM(lengths.shape, jnp.int32),
            pltpu.SMEM((migrate,), jnp.int32),
            pltpu.SMEM((heads,), jnp.int32),
            pltpu.VMEM(new_latent.shape, half),
            pltpu.VMEM((spare, lat), half),
            pltpu.VMEM((own, rows, lat), half),
            pltpu.VMEM((seqs, lines, lat), half),
            pltpu.VMEM((columns, lines, 2 * lat), half),
            pltpu.VMEM((heads, lines, 2 * lat), half),
            [pltpu.VMEM((heads, lines, size), half) for size in (KVR + 128, KVR)],
            [pltpu.VMEM((heads, lines, size), half) for size in (KVR + 128, KVR)],
            pltpu.VMEM((2, heads, columns * tokens, heads_each * VD), half),
            pltpu.VMEM(w_uv.shape, half),
            pltpu.VMEM(w_out.shape, half),
            [pltpu.VMEM((own + groups * CAP, rows, size), half) for _, size in CHUNKS],
            [pltpu.VMEM((groups, CAP, rows, size), half) for _, size in CHUNKS[:-1]]
            + [pltpu.VMEM((groups, rows, CAP * ROPE), half)],
            pltpu.VMEM((groups, rows, CAP * ROPE), half),
            pltpu.VMEM((columns, 2 * slots, rows, KVR), half),
            pltpu.VMEM((2, columns, 2, rows, 2 * ROPE), half),
            pltpu.VMEM((columns, 2 * slots, rows, ROPE), half),
            pltpu.VMEM((2, columns * width, KVR), half),
            pltpu.VMEM((2, columns * width, ROPE), half),
            pltpu.VMEM((columns, slots, rows, KVR), half),
            pltpu.VMEM((columns, 2, rows, 2 * ROPE), half),
            [pltpu.VMEM((columns, slots, rows, size), half) for _, size in CHUNKS[:-1]]
            + [pltpu.VMEM((columns, 2, rows, 2 * ROPE), half)],
            dma((count,)),
            dma((count,)),
            dma((2,)),
            dma((2,)),
            dma((2,)),
            dma((2,)),
            dma((count,)),
            dma((count,)),
            dma((2,)),
            dma((2,)),
            dma((2,)),
            dma((2, heads)),
            dma((9 + count,)),
        ],
        compiler_params=pltpu.CompilerParams(
            collective_id=0, has_side_effects=True, vmem_limit_bytes=48 * 1024 * 1024
        ),
    )(
        *(
            pltpu.with_memory_space_constraint(operand, pltpu.HBM)
            for operand in (
                jnp.transpose(mig_source, (0, 2, 1)),
                mig_page,
                page_table,
                lengths,
                old_pool,
                queries.reshape(seqs, lines, lat),
                new_latent,
                w_uv,
                w_out,
            )
        )
    )
    return result.reshape(seqs, tokens, features)


def solution(mesh):
    return jax.shard_map(
        shards,
        mesh=mesh,
        in_specs=(
            P("group", "head", None),
            P(),
            P(),
            P("group", None),
            P("group"),
            P("group", None, "head", None),
            P("group", None, None),
            P("head", None, None),
            P(None, "head"),
        ),
        out_specs=P("group", None, "head"),
        check_vma=False,
    )
```
